256 devices in a mesh: replica: 8 (over y, z_hi), fsdp: 32 (over x, z_lo, core).
Axes of the slice: x: 4, y: 4, z: 8 (z_hi: 2, z_lo: 4; z = z_hi * 4 + z_lo), core: 2. Of those that a mesh axis runs over, the one named last changes fastest.
Arguments:
- activations: bfloat16 [8, 4096, 8192], P('replica', 'fsdp'), may hold values from -18 to 18, as said below
- norm_gain: float32 [8, 8192], P('replica'), may hold values from 0.5 to 1.5
- key_weight: bfloat16 [8, 8192, 512], P('replica', 'fsdp'), may hold values from -0.0625 to 0.0625
- key_cotangent: bfloat16 [8, 4096, 512], P('replica', 'fsdp'), may hold values from -6 to 6
- local_fragment: float32 [8, 8192, 512], P('replica', 'fsdp'), may hold values from -6 to 6
- global_fragment: float32 [8192, 512], P('fsdp'), may hold values from -6 to 6
- momentum_codes: bfloat16 [8192, 512], P('fsdp'), may hold values from -1 to 1
- momentum_scales: float32 [8192, 4], P('fsdp'), may hold values from 0.05 to 0.5
Outputs:
- keys: float32 [8, 4096, 512], P('replica', 'fsdp')
- weight_grad: float32 [8, 8192, 512], P('replica', 'fsdp')
- gain_grad: float32 [8, 8192], P('replica', 'fsdp')
- input_gradient_rows: float32 [8, 4096, 8192], P('replica', 'fsdp')
- new_global: float32 [8192, 512], P('fsdp')
- new_codes: bfloat16 [8192, 512], P('fsdp')
- new_scales: float32 [8192, 4], P('fsdp')
The draws below stay inside these ranges and needn't reach their ends.
Inputs may be any that keep to these rules, and one draw needn't show every extreme that they name: Each token's activations carry their own scale, between 0.3 and 3 times that of the others in spread.
All inputs are finite; a program needn't handle non-finite values. Where the reference program divides by a largest or mean magnitude, that divisor is 1e-20 or more.
Results may differ from the reference program's by a relative error of at most 0.0029.
Values may be sent and summed in bfloat16 or wider, within the bound.
No kernel may reach another device: no remote copies, remote signals or barrier semaphores. Data moves between devices by JAX's collectives and lax.ppermute only.
A program may use at most 128 MiB of HBM per device.

```python
import math
import jax
import jax.numpy as jnp
from jax import lax

D = 8192
KV = 512
BLOCK = 128
TOKENS = 4096
N_REPLICA = 8


def draw_activations(key, part):
    key = jax.random.fold_in(key, 11)
    first, second = jax.random.split(key)
    base = jnp.clip(jax.random.normal(first, (N_REPLICA, TOKENS, D), jnp.float32), -6.0, 6.0)
    spread = jnp.exp(jax.random.uniform(second, (N_REPLICA, TOKENS, 1), jnp.float32, jnp.log(0.3), jnp.log(3.0)))
    return (base * spread).astype(jnp.bfloat16)


def block_levels(rng, shape, cuts, least, largest):
    gain, own = 1.0, jax.random.fold_in(rng, 6)
    for position, parts in cuts:
        heights = jnp.exp(jax.random.uniform(jax.random.fold_in(own, position), (parts,), jnp.float32, least / len(cuts), largest / len(cuts)))
        gain = gain * jnp.repeat(heights, shape[position] // parts).reshape([-1 if axis == position else 1 for axis in range(len(shape))])
    return gain


def centred(rng, dims, scale, bound, cuts=(), held_as=jnp.bfloat16):
    entries = scale * jax.random.normal(rng, dims, jnp.float32)
    if cuts:
        entries = entries * block_levels(rng, dims, cuts, -0.22, 0.18)
    return jnp.clip(entries, -bound, bound).astype(held_as)


def setup_inputs(seed: int = 0) -> dict:
    streams_of = jax.random.split(jax.random.key(seed), 9)
    activations = draw_activations(jax.random.fold_in(streams_of[8], 71), 0)
    norm_gain = jnp.clip(1.0 + 0.1 * jax.random.normal(streams_of[1], (N_REPLICA, D), jnp.float32), 0.5, 1.5)
    key_weight = centred(streams_of[2], (N_REPLICA, D, KV), D ** -0.5, 0.0625, ((0, 8), (1, 32)))
    key_cotangent = centred(streams_of[3], (N_REPLICA, TOKENS, KV), 1.0, 6.0, ((0, 8), (1, 32)))
    local_fragment = centred(streams_of[4], (N_REPLICA, D, KV), 1.0, 6.0, ((0, 8), (1, 32)), jnp.float32)
    global_fragment = centred(streams_of[5], (D, KV), 1.0, 6.0, ((0, 32),), jnp.float32)
    momentum_codes = jnp.clip(jax.random.uniform(streams_of[6], (D, KV), jnp.float32, -1.0, 1.0) * block_levels(streams_of[6], (D, KV), ((0, 32),), -0.4, 0.0), -1.0, 1.0).astype(jnp.bfloat16)
    momentum_scales = jnp.clip(jnp.exp(math.log(0.5) - 2.3025851 * jax.random.uniform(streams_of[7], (D, KV // BLOCK), jnp.float32) ** block_levels(streams_of[7], (D, KV // BLOCK), ((0, 32),), -0.2, 0.2)), 0.05, 0.5)
    return dict(activations=activations, norm_gain=norm_gain, key_weight=key_weight, key_cotangent=key_cotangent, local_fragment=local_fragment, global_fragment=global_fragment, momentum_codes=momentum_codes, momentum_scales=momentum_scales)


EPS = 1e-05
MU = 0.9
RATE = 0.7

def one_replica(items):
    acts, gain_vector, weight, grads = items
    input_float = acts.astype(jnp.float32)
    inverse_root_mean = lax.rsqrt(lax.optimization_barrier(jnp.mean(input_float * input_float, axis=-1, keepdims=True)) + EPS)
    centered_input = input_float * inverse_root_mean
    normalized_rows = (centered_input * gain_vector).astype(jnp.bfloat16)
    keys = jnp.dot(normalized_rows, weight, preferred_element_type=jnp.float32)
    wgrad = lax.dot_general(normalized_rows, grads, (((0,), (0,)), ((), ())), preferred_element_type=jnp.float32)
    normalized_cotangent = lax.dot_general(grads, weight, (((1,), (1,)), ((), ())), preferred_element_type=jnp.float32)
    gain_gradient = lax.optimization_barrier(jnp.sum(normalized_cotangent * centered_input, axis=0))
    centered_cotangent = normalized_cotangent * gain_vector
    inner_product = lax.optimization_barrier(jnp.mean(centered_cotangent * centered_input, axis=-1, keepdims=True))
    input_gradient = inverse_root_mean * (centered_cotangent - centered_input * inner_product)
    return (keys, wgrad, gain_gradient, input_gradient)

def outer_update(glob, pseudo, codes, scales):
    rows, width = glob.shape
    momentum = codes.astype(jnp.float32).reshape(rows, width // BLOCK, BLOCK) * scales[:, :, None]
    moved = MU * momentum + pseudo.reshape(rows, width // BLOCK, BLOCK)
    new_global = glob - RATE * (pseudo + MU * moved.reshape(rows, width))
    new_scales = lax.optimization_barrier(jnp.max(jnp.abs(moved), axis=-1)) + 1e-06
    new_codes = (moved / new_scales[:, :, None]).reshape(rows, width).astype(jnp.bfloat16)
    return (new_global, new_codes, new_scales)

def reference(activations, norm_gain, key_weight, key_cotangent, local_fragment, global_fragment, momentum_codes, momentum_scales):
    keys, wgrad, gain_gradient, input_gradient = lax.map(one_replica, (activations, norm_gain, key_weight, key_cotangent))
    pseudo = lax.optimization_barrier(jnp.sum(global_fragment[None] - local_fragment, axis=0)) / N_REPLICA
    new_global, new_codes, new_scales = outer_update(global_fragment, pseudo, momentum_codes, momentum_scales)
    return (keys, wgrad, gain_gradient, input_gradient, new_global, new_codes, new_scales)
```

```python
import functools

import jax
import jax.numpy as jnp
from jax import lax
from jax.experimental import pallas as pl
from jax.experimental.pallas import tpu as pltpu
from jax.sharding import PartitionSpec as P

EPS = 1e-05
MU = 0.9
RATE = 0.7
X, Z, C = 4, 4, 2
Y, H = 4, 2
OFFSETS = (0, 1, 3, 2)
FIRST = ((0, (0, 1), (0, 0), None), (1, (0,), (1, 0), None), (2, (0,), (1, 1), None))
SECOND = (
    (0, (2, 3), (0, 0), (1, 2)),
    (0, (0, 1), None, (1, 0)),
    (1, (0,), None, (1, 4)),
    (2, (0,), None, (1, 5)),
)
THIRD = ((1, (1, 2, 3), (0, 0), (1, 0)), (2, (1, 2, 3), (0, 3), (1, 3)))
LAST = ((3, (0, 1, 2, 3), (0, 0), (1, 0)),)
VMEM_LIMIT = 56 * 1024 * 1024
F32 = jnp.float32
BF16 = jnp.bfloat16


def index_of(x, z, c):
    return (x * Z + z) * C + c


def shift(value, dx=0, flip=0, swap=0):
    moves = [
        (index_of(x, z, c), index_of((x + dx) % X, z ^ flip, c ^ swap))
        for x in range(X)
        for z in range(Z)
        for c in range(C)
    ]
    return lax.ppermute(value, "fsdp", moves)


def trade(value, flip=0, far=0):
    moves = [(y * H + h, (y ^ flip) * H + (h ^ far)) for y in range(Y) for h in range(H)]
    return lax.ppermute(value, "replica", moves)


def params(**kw):
    return pltpu.CompilerParams(vmem_limit_bytes=VMEM_LIMIT, **kw)


def norm_kernel(place, acts, gain, cot, rinv, *slots):
    value = acts[...].astype(F32)
    inverse = lax.rsqrt(jnp.mean(value * value, axis=-1, keepdims=True) + EPS)
    rinv[...] = jnp.broadcast_to(inverse, rinv.shape)
    width = acts.shape[1] // X
    for step in range(X):
        start = pl.multiple_of(lax.rem(place[0] + step, X) * width, width)
        part = acts[:, pl.ds(start, width)].astype(F32) * inverse
        slots[step][:, :width] = (part * gain[:, pl.ds(start, width)]).astype(BF16)
        slots[step][:, width:] = cot[...]


def normalise(place, acts, gain, cot):
    tokens, width = acts.shape
    keys = cot.shape[1]
    rows = 32
    part = width // X + keys
    whole = lambda i, place: (0, 0)
    return pl.pallas_call(
        norm_kernel,
        grid_spec=pltpu.PrefetchScalarGridSpec(
            num_scalar_prefetch=1,
            grid=(tokens // rows,),
            in_specs=[
                pl.BlockSpec((rows, width), lambda i, place: (i, 0)),
                pl.BlockSpec((1, width), whole),
                pl.BlockSpec((rows, keys), lambda i, place: (i, 0)),
            ],
            out_specs=[pl.BlockSpec((rows, 128), lambda i, place: (i, 0))]
            + [pl.BlockSpec((rows, part), lambda i, place: (i, 0))] * X,
        ),
        out_shape=[jax.ShapeDtypeStruct((tokens, 128), F32)]
        + [jax.ShapeDtypeStruct((tokens, part), BF16)] * X,
        compiler_params=params(),
        name="normalise",
    )(place, acts, gain, cot)


def pack_kernel(span, place, r0, r1, r2, r3, features):
    tokens = r0.shape[0]
    width = Z * C * span
    for number, r in enumerate((r0, r1, r2, r3)):
        part = slice(number * tokens, (number + 1) * tokens)
        for flip in range(Z):
            start = (place[1] ^ flip) * (C * span) + (1 - place[2]) * span
            features[part, flip * span : (flip + 1) * span] = r[
                :, pl.ds(pl.multiple_of(start, span), span)
            ]
        features[part, Z * span :] = r[:, width:]


def pack(place, rows, span, keys):
    tokens = rows[0].shape[0] * X
    vmem = pl.BlockSpec(memory_space=pltpu.VMEM)
    return pl.pallas_call(
        functools.partial(pack_kernel, span),
        in_specs=[pl.BlockSpec(memory_space=pltpu.SMEM)] + [vmem] * X,
        out_specs=vmem,
        out_shape=jax.ShapeDtypeStruct((tokens, Z * span + keys), BF16),
        compiler_params=params(),
        name="pack",
    )(place, *rows)


def wgrad_kernel(place, r0, r1, r2, r3, other, kept, sent):
    span, keys = kept.shape[1:]
    width = Z * C * span
    mine = (r0, r1, r2, r3)
    cots = jnp.concatenate([r[:, width:] for r in mine] + [other[:, Z * span :]], axis=0)
    for flip in range(Z):
        start = pl.multiple_of((place[1] ^ flip) * (C * span) + place[2] * span, span)
        rows = jnp.concatenate(
            [r[:, pl.ds(start, span)] for r in mine]
            + [other[:, flip * span : (flip + 1) * span]],
            axis=0,
        )
        total = lax.dot_general(
            rows, cots, (((0,), (0,)), ((), ())), preferred_element_type=F32
        )
        if flip % 2:
            sent[flip // 2] = total.astype(BF16)
        else:
            kept[flip // 2] = total


def wgrad_part(place, rows, other, span, keys):
    vmem = pl.BlockSpec(memory_space=pltpu.VMEM)
    return pl.pallas_call(
        wgrad_kernel,
        in_specs=[pl.BlockSpec(memory_space=pltpu.SMEM)] + [vmem] * (X + 1),
        out_specs=[vmem] * 2,
        out_shape=[
            jax.ShapeDtypeStruct((2, span, keys), F32),
            jax.ShapeDtypeStruct((2, span, keys), BF16),
        ],
        compiler_params=params(),
        name="wgrad_part",
    )(place, *rows, other)


def pieces_of(layout, refs, place, part):
    span = part // (Z * C)
    pieces = []
    for slot, flips, *sources in layout:
        block = lax.rem(place[0] + OFFSETS[slot], X)
        for source, which in zip(sources, (place[2], 1 - place[2])):
            if source is None:
                continue
            number, first = source
            for row, flip in enumerate(flips, first):
                local = pl.multiple_of((place[1] ^ flip) * (C * span) + which * span, span)
                start = pl.multiple_of(block * part + local, span)
                rows = slice(row * span, (row + 1) * span)
                pieces.append((slot, start, local, refs[number], rows))
    return pieces


def keys_sum(pieces, acts, gain, inverse):
    total = None
    for _, start, _, ref, rows in pieces:
        lanes = pl.ds(start, rows.stop - rows.start)
        hat = acts[:, lanes].astype(F32) * inverse
        normed = (hat * gain[:, lanes]).astype(BF16)
        term = jnp.dot(normed, ref[rows, :], preferred_element_type=F32)
        total = term if total is None else total + term
    return total


def cotangent_of(cots, ref, rows):
    return lax.dot_general(
        cots, ref[rows, :], (((1,), (1,)), ((), ())), preferred_element_type=F32
    )


def early_kernel(layout, started, place, acts, gain, rinv, cot, *refs):
    weights, (keys, scaled) = refs[started:-2], refs[-2:]
    part = acts.shape[1] // X
    inverse = rinv[:, :1]
    pieces = pieces_of(layout, weights, place, part)
    total = keys_sum(pieces, acts, gain, inverse)
    keys[...] = refs[0][...] + total if started else total
    cots = cot[...]
    for number, (_, start, _, ref, rows) in enumerate(pieces):
        span = rows.stop - rows.start
        scaled[number] = inverse * cotangent_of(cots, ref, rows) * gain[:, pl.ds(start, span)]


def backward_early(place, acts, gain, rinv, cot, before, layout, weights):
    tokens, width = acts.shape
    span = width // (X * Z * C)
    pieces = sum(len(flips) * (2 - sources.count(None)) for _, flips, *sources in layout)
    vmem = pl.BlockSpec(memory_space=pltpu.VMEM)
    return pl.pallas_call(
        functools.partial(early_kernel, layout, len(before)),
        in_specs=[pl.BlockSpec(memory_space=pltpu.SMEM)]
        + [vmem] * (4 + len(before) + len(weights)),
        out_specs=[vmem, vmem],
        out_shape=[
            jax.ShapeDtypeStruct((tokens, cot.shape[1]), F32),
            jax.ShapeDtypeStruct((pieces, tokens, span), F32),
        ],
        compiler_params=params(),
        name="backward_early",
    )(place, acts, gain, rinv, cot, *before, *weights)


def late_kernel(
    layout, done, place, acts, gain, rinv, cot, early, *refs
):
    sources, refs = refs[: len(done)], refs[len(done) :]
    weights, (keys, dx, held, arrive, leave) = refs[:-5], refs[-5:]
    tokens, width = acts.shape
    part = width // X
    loads = [[] for _ in range(X)]
    count = 0
    for source, entries in zip(sources, done):
        for number, (slot, _, local, _, rows) in enumerate(
            pieces_of(entries, [None] * 16, place, part)
        ):
            load = pltpu.make_async_copy(
                source.at[number],
                held.at[slot, :, pl.ds(local, rows.stop - rows.start)],
                arrive.at[count],
            )
            load.start()
            loads[slot].append(load)
            count += 1
    inverse = rinv[:, :1]
    pieces = pieces_of(layout, weights, place, part)
    total = early[...] + keys_sum(pieces, acts, gain, inverse)
    keys[...] = total
    cots = cot[...]
    inner = jnp.sum(total * cots.astype(F32), axis=-1, keepdims=True) / width
    factor = inverse * inverse * inner

    def send(slot):
        start = pl.multiple_of(lax.rem(place[0] + OFFSETS[slot], X) * part, part)
        copy = pltpu.make_async_copy(held.at[slot], dx.at[:, pl.ds(start, part)], leave.at[slot])
        copy.start()
        return copy

    copies = []
    for slot in range(X - 1):
        for load in loads[slot]:
            load.wait()
        start = pl.multiple_of(lax.rem(place[0] + OFFSETS[slot], X) * part, part)
        held[slot] = held[slot] - acts[:, pl.ds(start, part)].astype(F32) * factor
        copies.append(send(slot))
    for slot, start, local, ref, rows in pieces:
        span = rows.stop - rows.start
        lanes = pl.ds(start, span)
        held[slot, :, pl.ds(local, span)] = (
            inverse * cotangent_of(cots, ref, rows) * gain[:, lanes]
            - acts[:, lanes].astype(F32) * factor
        )
    copies.append(send(X - 1))
    for copy in copies:
        copy.wait()


def backward_late(place, acts, gain, rinv, cot, early, sources, done, layout, weights):
    tokens, width = acts.shape
    vmem = pl.BlockSpec(memory_space=pltpu.VMEM)
    hbm = pl.BlockSpec(memory_space=pl.ANY)
    return pl.pallas_call(
        functools.partial(late_kernel, layout, done),
        in_specs=[pl.BlockSpec(memory_space=pltpu.SMEM)]
        + [vmem] * 5
        + [hbm] * len(sources)
        + [vmem] * len(weights),
        out_specs=[vmem, hbm],
        out_shape=[
            jax.ShapeDtypeStruct((tokens, cot.shape[1]), F32),
            jax.ShapeDtypeStruct((tokens, width), F32),
        ],
        scratch_shapes=[
            pltpu.VMEM((X, tokens, width // X), F32),
            pltpu.SemaphoreType.DMA((sum(source.shape[0] for source in sources),)),
            pltpu.SemaphoreType.DMA((X,)),
        ],
        compiler_params=params(),
        name="backward_late",
    )(place, acts, gain, rinv, cot, early, *sources, *weights)


def delta_kernel(place, glob, local, keep, send):
    rows = keep.shape[1]
    for flip, out, row in ((0, keep, 0), (3, keep, 1), (1, send, 0), (2, send, 1)):
        part = pl.ds(pl.multiple_of((place[3] ^ flip) * rows, rows), rows)
        out[row] = glob[part, :] - local[part, :]


def delta(place, glob, local):
    rows, width = glob.shape
    vmem = pl.BlockSpec(memory_space=pltpu.VMEM)
    return pl.pallas_call(
        delta_kernel,
        in_specs=[pl.BlockSpec(memory_space=pltpu.SMEM), vmem, vmem],
        out_specs=[vmem, vmem],
        out_shape=[jax.ShapeDtypeStruct((2, rows // Y, width), F32)] * 2,
        compiler_params=params(),
        name="delta",
    )(place, glob, local)


def outer_kernel(place, p0, p1, p2, p3, glob, codes, scales, new_global, new_codes, new_scales):
    rows = p0.shape[0]
    blocks = scales.shape[0]
    span = p0.shape[1] // blocks
    columns = jnp.concatenate([scales[...]] * (128 // blocks), axis=0).T
    spread = 128 // blocks
    for flip, part in enumerate((p0, p1, p2, p3)):
        start = pl.multiple_of((place[3] ^ flip) * rows, rows)
        new_global[pl.ds(start, rows), :] = part[...]
    maxima = []
    for block in range(blocks):
        lanes = slice(block * span, (block + 1) * span)
        pseudo = new_global[:, lanes]
        momentum = codes[:, lanes].astype(F32) * columns[:, block : block + 1]
        moved = MU * momentum + pseudo
        new_global[:, lanes] = glob[:, lanes] - RATE * (pseudo + MU * moved)
        scale = jnp.max(jnp.abs(moved), axis=-1, keepdims=True) + 1e-06
        new_codes[:, lanes] = (moved / scale).astype(BF16)
        maxima.append(jnp.broadcast_to(scale, (Y * rows, spread)))
    across = jnp.concatenate(maxima, axis=-1).T
    new_scales[...] = jnp.concatenate(
        [across[start : start + 1] for start in range(0, 128, spread)], axis=0
    )


def outer_update(place, parts, glob, codes, scales):
    vmem = pl.BlockSpec(memory_space=pltpu.VMEM)
    new_global, new_codes, new_scales = pl.pallas_call(
        outer_kernel,
        in_specs=[pl.BlockSpec(memory_space=pltpu.SMEM)] + [vmem] * (Y + 3),
        out_specs=[vmem] * 3,
        out_shape=[
            jax.ShapeDtypeStruct(glob.shape, F32),
            jax.ShapeDtypeStruct(codes.shape, BF16),
            jax.ShapeDtypeStruct(scales.shape[::-1], F32),
        ],
        compiler_params=params(),
        name="outer_update",
    )(place, *parts, glob, codes, scales.T)
    return new_global, new_codes, new_scales.T


def together(*values):
    return lax.optimization_barrier(values)


def body(
    activations,
    norm_gain,
    key_weight,
    key_cotangent,
    local_fragment,
    global_fragment,
    momentum_codes,
    momentum_scales,
):
    acts, weight, cot = activations[0], key_weight[0], key_cotangent[0]
    here, replica = lax.axis_index("fsdp"), lax.axis_index("replica")
    place = jnp.stack([here // (Z * C), (here // C) % Z, here % C, replica // H]).astype(jnp.int32)
    span = weight.shape[0]

    width = cot.shape[1]
    second = shift(weight, flip=1)
    near3, near1 = shift(weight, dx=1), shift(weight, dx=-1)
    rinv, *slots = normalise(place, acts, norm_gain, cot)
    *slots, second, near3, near1, glob = together(*slots, second, near3, near1, global_fragment)

    rows = [slots[0]] + [shift(slots[d], dx=d) for d in (1, 3, 2)]
    pair = jnp.concatenate([weight, second], axis=0)
    third = shift(pair, flip=2)
    near = jnp.concatenate([near1, near3], axis=0)
    keep, send = delta(place, glob, local_fragment[0])
    keep = keep + trade(send, flip=1)
    came = trade(keep[1], flip=3)
    early, first = backward_early(place, acts, norm_gain, rinv, cot, (), FIRST, (pair, near))
    *rows, third, came, early = together(*rows, third, came, early)

    rest = jnp.concatenate([second, third], axis=0)
    far3, far1 = shift(rest, dx=1), shift(rest, dx=-1)
    total = keep[0] + came
    other = shift(pack(place, rows, span, width), swap=1)
    kept, sent = wgrad_part(place, rows, other, span, width)
    base = jnp.concatenate([pair, third, near], axis=0)
    base_mate = shift(base, swap=1)
    early, sent = together(early, sent)
    early, second_part = backward_early(
        place, acts, norm_gain, rinv, cot, (early,), SECOND, (third, base_mate)
    )
    back = shift(sent, flip=1)
    far3, far1, back, early, total = together(far3, far1, back, early, total)

    across_a = shift(jnp.concatenate([near1, far1[:span]], axis=0), dx=-1)
    across_b = shift(far3[span:], dx=1)
    far = jnp.concatenate([far1, far3], axis=0)
    far_mate = shift(far, swap=1)
    last = (kept[1] + back[1].astype(F32)).astype(BF16)
    end = shift(last, flip=2)
    came = trade(total, far=1)
    early, third_part = backward_early(
        place, acts, norm_gain, rinv, cot, (early,), THIRD, (far, far_mate)
    )
    across_a, across_b, early, end, came = together(across_a, across_b, early, end, came)
    across = jnp.concatenate([across_a, across_b], axis=0)
    across_mate = shift(across, swap=1)
    pseudo = (total + came) / (Y * H)
    parts = [pseudo] + [trade(pseudo, flip=flip) for flip in range(1, Y)]
    weight_grad = kept[0] + back[0].astype(F32) + end.astype(F32)
    gain_here = lax.dynamic_slice_in_dim(norm_gain[0], here * span, span)
    gain_grad = jnp.sum(weight.astype(F32) * weight_grad, axis=-1) / gain_here
    across_mate, gain_grad = together(across_mate, gain_grad)
    keys, input_gradient_rows = backward_late(
        place, acts, norm_gain, rinv, cot, early, (first, second_part, third_part),
        (FIRST, SECOND, THIRD), LAST, (across, across_mate),
    )
    keys, *parts = together(keys, *parts)
    new_global, new_codes, new_scales = outer_update(
        place, parts, global_fragment, momentum_codes, momentum_scales
    )
    return (
        keys[None],
        weight_grad[None],
        gain_grad[None],
        input_gradient_rows[None],
        new_global,
        new_codes,
        new_scales,
    )


def solution(mesh):
    in_specs = (
        P("replica", "fsdp", None),
        P("replica", None),
        P("replica", "fsdp", None),
        P("replica", "fsdp", None),
        P("replica", "fsdp", None),
        P("fsdp", None),
        P("fsdp", None),
        P("fsdp", None),
    )
    out_specs = (
        P("replica", "fsdp", None),
        P("replica", "fsdp", None),
        P("replica", "fsdp"),
        P("replica", "fsdp", None),
        P("fsdp", None),
        P("fsdp", None),
        P("fsdp", None),
    )
    return jax.shard_map(body, mesh=mesh, in_specs=in_specs, out_specs=out_specs, check_vma=False)
```

```python
import functools

import jax
import jax.numpy as jnp
from jax import lax
from jax.experimental import pallas as pl
from jax.experimental.pallas import tpu as pltpu
from jax.sharding import PartitionSpec as P

EPS = 1e-05
MU = 0.9
RATE = 0.7
X, Z, C = 4, 4, 2
Y, H = 4, 2
OFFSETS = (0, 1, 3, 2)
FIRST = (
    (0, (0,), (0, 0), None),
    (0, (1,), (1, 0), None),
    (1, (0,), (2, 0), None),
    (2, (0,), (3, 0), None),
)
SECOND = (
    (0, (2, 3), (0, 0), (2, 0)),
    (0, (0, 1), None, (1, 0)),
    (1, (0,), None, (1, 2)),
    (2, (0,), None, (1, 3)),
)
THIRD = ((1, (1, 2, 3), (0, 0), (1, 0)), (2, (1, 2, 3), (0, 3), (1, 3)))
LAST = ((3, (0, 1), (0, 0), (1, 0)), (3, (2, 3), (2, 0), (3, 0)))
VMEM_LIMIT = 56 * 1024 * 1024
F32 = jnp.float32
BF16 = jnp.bfloat16


def index_of(x, z, c):
    return (x * Z + z) * C + c


def shift(value, dx=0, flip=0, swap=0):
    moves = [
        (index_of(x, z, c), index_of((x + dx) % X, z ^ flip, c ^ swap))
        for x in range(X)
        for z in range(Z)
        for c in range(C)
    ]
    return lax.ppermute(value, "fsdp", moves)


def trade(value, flip=0, far=0):
    moves = [(y * H + h, (y ^ flip) * H + (h ^ far)) for y in range(Y) for h in range(H)]
    return lax.ppermute(value, "replica", moves)


def params(**kw):
    return pltpu.CompilerParams(vmem_limit_bytes=VMEM_LIMIT, **kw)


def norm_kernel(place, acts, gain, cot, rinv, *slots):
    value = acts[...].astype(F32)
    inverse = lax.rsqrt(jnp.mean(value * value, axis=-1, keepdims=True) + EPS)
    rinv[...] = jnp.broadcast_to(inverse, rinv.shape)
    width = acts.shape[1] // X
    span = width // (Z * C)
    for step in range(X):
        base = lax.rem(place[0] + step, X) * width
        for number in range(Z * C):
            core, flip = number // Z, number % Z
            local = (place[1] ^ flip) * (C * span) + (place[2] ^ core) * span
            lanes = pl.ds(pl.multiple_of(base + local, span), span)
            part = acts[:, lanes].astype(F32) * inverse
            slots[step][:, number * span : (number + 1) * span] = (part * gain[:, lanes]).astype(BF16)
        slots[step][:, width:] = cot[...]


def normalise(place, acts, gain, cot):
    tokens, width = acts.shape
    keys = cot.shape[1]
    rows = 64
    part = width // X + keys
    whole = lambda i, place: (0, 0)
    return pl.pallas_call(
        norm_kernel,
        grid_spec=pltpu.PrefetchScalarGridSpec(
            num_scalar_prefetch=1,
            grid=(tokens // rows,),
            in_specs=[
                pl.BlockSpec((rows, width), lambda i, place: (i, 0)),
                pl.BlockSpec((1, width), whole),
                pl.BlockSpec((rows, keys), lambda i, place: (i, 0)),
            ],
            out_specs=[pl.BlockSpec((rows, 128), lambda i, place: (i, 0))]
            + [pl.BlockSpec((rows, part), lambda i, place: (i, 0))] * X,
        ),
        out_shape=[jax.ShapeDtypeStruct((tokens, 128), F32)]
        + [jax.ShapeDtypeStruct((tokens, part), BF16)] * X,
        compiler_params=params(),
        name="normalise",
    )(place, acts, gain, cot)


def pack_kernel(r0, r1, r2, r3, second, third, features, rest, wide, blocks, arrive, leave):
    tokens = r0.shape[0]
    skip = r0.shape[1] - features.shape[1]
    span = second.shape[0]
    moves = [
        (second, blocks.at[pl.ds(0, span)], rest.at[pl.ds(0, span)]),
        (third, blocks.at[pl.ds(span, third.shape[0])], rest.at[pl.ds(span, third.shape[0])]),
    ]
    for number, r in enumerate((r0, r1, r2, r3)):
        part = pl.ds(number * tokens, tokens)
        moves.append((r.at[:, pl.ds(skip, features.shape[1])], wide.at[part], features.at[part]))
    loads = [pltpu.make_async_copy(m[0], m[1], arrive.at[i]) for i, m in enumerate(moves)]
    stores = [pltpu.make_async_copy(m[1], m[2], leave.at[i]) for i, m in enumerate(moves)]
    for load in loads:
        load.start()
    for load, store in zip(loads, stores):
        load.wait()
        store.start()
    for store in stores:
        store.wait()


def pack(rows, second, third, span):
    tokens, width = rows[0].shape
    hbm = pl.BlockSpec(memory_space=pl.ANY)
    shapes = [
        (X * tokens, width - Z * span),
        (second.shape[0] + third.shape[0], second.shape[1]),
    ]
    return pl.pallas_call(
        pack_kernel,
        in_specs=[hbm] * (X + 2),
        out_specs=[hbm] * 2,
        out_shape=[jax.ShapeDtypeStruct(shape, BF16) for shape in shapes],
        scratch_shapes=[pltpu.VMEM(shape, BF16) for shape in shapes]
        + [pltpu.SemaphoreType.DMA((X + 2,))] * 2,
        compiler_params=params(),
        name="pack",
    )(*rows, second, third)


def wgrad_kernel(r0, r1, r2, r3, other, kept, sent1, sent3):
    span = kept.shape[1]
    own, width = Z * span, Z * C * span
    mine = (r0, r1, r2, r3)
    cots = jnp.concatenate([r[:, width:] for r in mine] + [other[:, own:]], axis=0)
    for flip in range(Z):
        lanes = slice(flip * span, (flip + 1) * span)
        rows = jnp.concatenate([r[:, lanes] for r in mine] + [other[:, lanes]], axis=0)
        total = lax.dot_general(
            rows, cots, (((0,), (0,)), ((), ())), preferred_element_type=F32
        )
        if flip % 2:
            (sent3 if flip == 3 else sent1)[...] = total.astype(BF16)
        else:
            kept[flip // 2] = total


def wgrad_part(rows, other, span, keys):
    vmem = pl.BlockSpec(memory_space=pltpu.VMEM)
    return pl.pallas_call(
        wgrad_kernel,
        in_specs=[vmem] * (X + 1),
        out_specs=[vmem] * 3,
        out_shape=[
            jax.ShapeDtypeStruct((2, span, keys), F32),
            jax.ShapeDtypeStruct((span, keys), BF16),
            jax.ShapeDtypeStruct((span, keys), BF16),
        ],
        compiler_params=params(),
        name="wgrad_part",
    )(*rows, other)


def pieces_of(layout, refs, place, part):
    span = part // (Z * C)
    pieces = []
    for slot, flips, *sources in layout:
        block = lax.rem(place[0] + OFFSETS[slot], X)
        for source, which in zip(sources, (place[2], 1 - place[2])):
            if source is None:
                continue
            number, first = source
            for row, flip in enumerate(flips, first):
                local = pl.multiple_of((place[1] ^ flip) * (C * span) + which * span, span)
                start = pl.multiple_of(block * part + local, span)
                rows = slice(row * span, (row + 1) * span)
                pieces.append((slot, start, local, refs[number], rows))
    return pieces


def keys_sum(pieces, acts, gain, inverse):
    total = None
    for _, start, _, ref, rows in pieces:
        lanes = pl.ds(start, rows.stop - rows.start)
        hat = acts[:, lanes].astype(F32) * inverse
        normed = (hat * gain[:, lanes]).astype(BF16)
        term = jnp.dot(normed, ref[rows, :], preferred_element_type=F32)
        total = term if total is None else total + term
    return total


def cotangent_of(cots, ref, rows):
    return lax.dot_general(
        cots, ref[rows, :], (((1,), (1,)), ((), ())), preferred_element_type=F32
    )


def early_kernel(layout, started, hold, place, acts, gain, rinv, cot, *refs):
    weights, (keys, scaled) = refs[started : -2 - hold], refs[-2 - hold :][:2]
    if hold:
        span = weights[0].shape[0]
        for number, ref in enumerate(weights):
            refs[-1][number * span : (number + 1) * span, :] = ref[...]
    part = acts.shape[1] // X
    inverse = rinv[:, :1]
    pieces = pieces_of(layout, weights, place, part)
    total = keys_sum(pieces, acts, gain, inverse)
    keys[...] = refs[0][...] + total if started else total
    cots = cot[...]
    for number, (_, start, _, ref, rows) in enumerate(pieces):
        span = rows.stop - rows.start
        scaled[number] = inverse * cotangent_of(cots, ref, rows) * gain[:, pl.ds(start, span)]


def backward_early(place, acts, gain, rinv, cot, before, layout, weights, hold=0):
    tokens, width = acts.shape
    span = width // (X * Z * C)
    pieces = sum(len(flips) * (2 - sources.count(None)) for _, flips, *sources in layout)
    vmem = pl.BlockSpec(memory_space=pltpu.VMEM)
    return pl.pallas_call(
        functools.partial(early_kernel, layout, len(before), hold),
        in_specs=[pl.BlockSpec(memory_space=pltpu.SMEM)]
        + [vmem] * (4 + len(before) + len(weights)),
        out_specs=[vmem] * (2 + hold),
        out_shape=[
            jax.ShapeDtypeStruct((tokens, cot.shape[1]), F32),
            jax.ShapeDtypeStruct((pieces, tokens, span), F32),
        ]
        + [jax.ShapeDtypeStruct((len(weights) * span, cot.shape[1]), BF16)] * hold,
        compiler_params=params(),
        name="backward_early",
    )(place, acts, gain, rinv, cot, *before, *weights)


def late_kernel(
    layout, done, place, acts, gain, rinv, cot, early, *refs
):
    sources, refs = refs[: len(done)], refs[len(done) :]
    weights, (keys, dx, held, arrive, leave) = refs[:-5], refs[-5:]
    tokens, width = acts.shape
    part = width // X
    loads = [[] for _ in range(X)]
    count = 0
    for source, entries in zip(sources, done):
        for number, (slot, _, local, _, rows) in enumerate(
            pieces_of(entries, [None] * 16, place, part)
        ):
            load = pltpu.make_async_copy(
                source.at[number],
                held.at[slot, :, pl.ds(local, rows.stop - rows.start)],
                arrive.at[count],
            )
            load.start()
            loads[slot].append(load)
            count += 1
    inverse = rinv[:, :1]
    pieces = pieces_of(layout, weights, place, part)
    total = early[...] + keys_sum(pieces, acts, gain, inverse)
    keys[...] = total
    cots = cot[...]
    inner = jnp.sum(total * cots.astype(F32), axis=-1, keepdims=True) / width
    factor = inverse * inverse * inner

    def send(slot):
        start = pl.multiple_of(lax.rem(place[0] + OFFSETS[slot], X) * part, part)
        copy = pltpu.make_async_copy(held.at[slot], dx.at[:, pl.ds(start, part)], leave.at[slot])
        copy.start()
        return copy

    copies = []
    for slot in range(X - 1):
        for load in loads[slot]:
            load.wait()
        start = pl.multiple_of(lax.rem(place[0] + OFFSETS[slot], X) * part, part)
        held[slot] = held[slot] - acts[:, pl.ds(start, part)].astype(F32) * factor
        copies.append(send(slot))
    for slot, start, local, ref, rows in pieces:
        span = rows.stop - rows.start
        lanes = pl.ds(start, span)
        held[slot, :, pl.ds(local, span)] = (
            inverse * cotangent_of(cots, ref, rows) * gain[:, lanes]
            - acts[:, lanes].astype(F32) * factor
        )
    copies.append(send(X - 1))
    for copy in copies:
        copy.wait()


def backward_late(place, acts, gain, rinv, cot, early, sources, done, layout, weights):
    tokens, width = acts.shape
    vmem = pl.BlockSpec(memory_space=pltpu.VMEM)
    hbm = pl.BlockSpec(memory_space=pl.ANY)
    return pl.pallas_call(
        functools.partial(late_kernel, layout, done),
        in_specs=[pl.BlockSpec(memory_space=pltpu.SMEM)]
        + [vmem] * 5
        + [hbm] * len(sources)
        + [vmem] * len(weights),
        out_specs=[vmem, hbm],
        out_shape=[
            jax.ShapeDtypeStruct((tokens, cot.shape[1]), F32),
            jax.ShapeDtypeStruct((tokens, width), F32),
        ],
        scratch_shapes=[
            pltpu.VMEM((X, tokens, width // X), F32),
            pltpu.SemaphoreType.DMA((sum(source.shape[0] for source in sources),)),
            pltpu.SemaphoreType.DMA((X,)),
        ],
        compiler_params=params(),
        name="backward_late",
    )(place, acts, gain, rinv, cot, early, *sources, *weights)


def delta_kernel(place, glob, local, keep, send):
    rows = keep.shape[1]
    for flip, out, row in ((0, keep, 0), (3, keep, 1), (1, send, 0), (2, send, 1)):
        part = pl.ds(pl.multiple_of((place[3] ^ flip) * rows, rows), rows)
        out[row] = glob[part, :] - local[part, :]


def delta(place, glob, local):
    rows, width = glob.shape
    vmem = pl.BlockSpec(memory_space=pltpu.VMEM)
    return pl.pallas_call(
        delta_kernel,
        in_specs=[pl.BlockSpec(memory_space=pltpu.SMEM), vmem, vmem],
        out_specs=[vmem, vmem],
        out_shape=[jax.ShapeDtypeStruct((2, rows // Y, width), F32)] * 2,
        compiler_params=params(),
        name="delta",
    )(place, glob, local)


def outer_kernel(place, p0, p1, p2, p3, glob, codes, scales, new_global, new_codes, new_scales):
    rows = p0.shape[0]
    blocks = scales.shape[0]
    span = p0.shape[1] // blocks
    columns = jnp.concatenate([scales[...]] * (128 // blocks), axis=0).T
    spread = 128 // blocks
    for flip, part in enumerate((p0, p1, p2, p3)):
        start = pl.multiple_of((place[3] ^ flip) * rows, rows)
        new_global[pl.ds(start, rows), :] = part[...]
    maxima = []
    for block in range(blocks):
        lanes = slice(block * span, (block + 1) * span)
        pseudo = new_global[:, lanes]
        momentum = codes[:, lanes].astype(F32) * columns[:, block : block + 1]
        moved = MU * momentum + pseudo
        new_global[:, lanes] = glob[:, lanes] - RATE * (pseudo + MU * moved)
        scale = jnp.max(jnp.abs(moved), axis=-1, keepdims=True) + 1e-06
        new_codes[:, lanes] = (moved / scale).astype(BF16)
        maxima.append(jnp.broadcast_to(scale, (Y * rows, spread)))
    across = jnp.concatenate(maxima, axis=-1).T
    new_scales[...] = jnp.concatenate(
        [across[start : start + 1] for start in range(0, 128, spread)], axis=0
    )


def outer_update(place, parts, glob, codes, scales):
    vmem = pl.BlockSpec(memory_space=pltpu.VMEM)
    new_global, new_codes, new_scales = pl.pallas_call(
        outer_kernel,
        in_specs=[pl.BlockSpec(memory_space=pltpu.SMEM)] + [vmem] * (Y + 3),
        out_specs=[vmem] * 3,
        out_shape=[
            jax.ShapeDtypeStruct(glob.shape, F32),
            jax.ShapeDtypeStruct(codes.shape, BF16),
            jax.ShapeDtypeStruct(scales.shape[::-1], F32),
        ],
        compiler_params=params(),
        name="outer_update",
    )(place, *parts, glob, codes, scales.T)
    return new_global, new_codes, new_scales.T


def together(*values):
    return lax.optimization_barrier(values)


def body(
    activations,
    norm_gain,
    key_weight,
    key_cotangent,
    local_fragment,
    global_fragment,
    momentum_codes,
    momentum_scales,
):
    acts, weight, cot = activations[0], key_weight[0], key_cotangent[0]
    here, replica = lax.axis_index("fsdp"), lax.axis_index("replica")
    place = jnp.stack([here // (Z * C), (here // C) % Z, here % C, replica // H]).astype(jnp.int32)
    span = weight.shape[0]

    width = cot.shape[1]
    second = shift(weight, flip=1)
    near3, near1 = shift(weight, dx=1), shift(weight, dx=-1)
    rinv, *slots = normalise(place, acts, norm_gain, cot)
    *slots, second, near3, near1, glob = together(*slots, second, near3, near1, global_fragment)

    rows = [slots[0]] + [shift(slots[d], dx=d) for d in (1, 3, 2)]
    third = shift(jnp.concatenate([weight, second], axis=0), flip=2)
    keep, send = delta(place, glob, local_fragment[0])
    keep = keep + trade(send, flip=1)
    came = trade(keep[1], flip=3)
    early, first, hold = backward_early(
        place, acts, norm_gain, rinv, cot, (), FIRST, (weight, second, near1, near3), hold=1
    )
    *rows, third, came, early = together(*rows, third, came, early)

    other, rest = pack(rows, second, third, span)
    other = shift(other, swap=1)
    far3, far1 = shift(rest, dx=1), shift(rest, dx=-1)
    total = keep[0] + came
    kept, sent1, sent3 = wgrad_part(rows, other, span, width)
    hold_mate, third_mate = shift(hold, swap=1), shift(third, swap=1)
    early, sent1 = together(early, sent1)
    early, second_part = backward_early(
        place, acts, norm_gain, rinv, cot, (early,), SECOND, (third, hold_mate, third_mate)
    )
    back3 = shift(sent3, flip=1)
    far3, far1, early, total, back3 = together(far3, far1, early, total, back3)

    across_a = shift(jnp.concatenate([near1, far1[:span]], axis=0), dx=-1)
    across_b = shift(far3[span:], dx=1)
    far = jnp.concatenate([far1, far3], axis=0)
    far_mate = shift(far, swap=1)
    came = trade(total, far=1)
    last = (kept[1] + back3.astype(F32)).astype(BF16)
    end = shift(last, flip=2)
    back1 = shift(sent1, flip=1)
    early, third_part = backward_early(
        place, acts, norm_gain, rinv, cot, (early,), THIRD, (far, far_mate)
    )
    early, end, back1 = together(early, end, back1)
    weight_grad = kept[0] + back1.astype(F32) + end.astype(F32)
    gain_here = lax.dynamic_slice_in_dim(norm_gain[0], here * span, span)
    gain_grad = jnp.sum(weight.astype(F32) * weight_grad, axis=-1) / gain_here
    across_a, across_b, early, gain_grad, came = together(across_a, across_b, early, gain_grad, came)
    mate_a, mate_b = shift(across_a, swap=1), shift(across_b, swap=1)
    pseudo = (total + came) / (Y * H)
    parts = [pseudo] + [trade(pseudo, flip=flip) for flip in range(1, Y)]
    keys, input_gradient_rows = backward_late(
        place, acts, norm_gain, rinv, cot, early, (first, second_part, third_part),
        (FIRST, SECOND, THIRD), LAST, (across_a, mate_a, across_b, mate_b),
    )
    keys, *parts = together(keys, *parts)
    new_global, new_codes, new_scales = outer_update(
        place, parts, global_fragment, momentum_codes, momentum_scales
    )
    return (
        keys[None],
        weight_grad[None],
        gain_grad[None],
        input_gradient_rows[None],
        new_global,
        new_codes,
        new_scales,
    )


def solution(mesh):
    in_specs = (
        P("replica", "fsdp", None),
        P("replica", None),
        P("replica", "fsdp", None),
        P("replica", "fsdp", None),
        P("replica", "fsdp", None),
        P("fsdp", None),
        P("fsdp", None),
        P("fsdp", None),
    )
    out_specs = (
        P("replica", "fsdp", None),
        P("replica", "fsdp", None),
        P("replica", "fsdp"),
        P("replica", "fsdp", None),
        P("fsdp", None),
        P("fsdp", None),
        P("fsdp", None),
    )
    return jax.shard_map(body, mesh=mesh, in_specs=in_specs, out_specs=out_specs, check_vma=False)
```

```python
import functools

import jax
import jax.numpy as jnp
from jax import lax
from jax.experimental import pallas as pl
from jax.experimental.pallas import tpu as pltpu
from jax.sharding import PartitionSpec as P

EPS = 1e-05
MU = 0.9
RATE = 0.7
X, Z, C = 4, 4, 2
Y, H = 4, 2
OFFSETS = (0, 1, 3, 2)
FIRST = (
    (0, (0,), (0, 0), None),
    (0, (1,), (1, 0), None),
    (1, (0,), (2, 0), None),
    (2, (0,), (3, 0), None),
)
SECOND = (
    (0, (2, 3), (0, 0), (1, 4)),
    (0, (0, 1), None, (1, 0)),
    (1, (0,), None, (1, 2)),
    (2, (0,), None, (1, 3)),
)
THIRD = ((1, (1, 2, 3), (0, 0), (1, 0)), (2, (1, 2, 3), (0, 3), (1, 3)))
LAST = ((3, (0, 1), (0, 0), (1, 0)), (3, (2, 3), (2, 0), (3, 0)))
VMEM_LIMIT = 56 * 1024 * 1024
F32 = jnp.float32
BF16 = jnp.bfloat16


def index_of(x, z, c):
    return (x * Z + z) * C + c


def shift(value, dx=0, flip=0, swap=0):
    moves = [
        (index_of(x, z, c), index_of((x + dx) % X, z ^ flip, c ^ swap))
        for x in range(X)
        for z in range(Z)
        for c in range(C)
    ]
    return lax.ppermute(value, "fsdp", moves)


def trade(value, flip=0, far=0):
    moves = [(y * H + h, (y ^ flip) * H + (h ^ far)) for y in range(Y) for h in range(H)]
    return lax.ppermute(value, "replica", moves)


def params(**kw):
    return pltpu.CompilerParams(vmem_limit_bytes=VMEM_LIMIT, **kw)


def norm_kernel(place, acts, gain, cot, rinv, *slots):
    value = acts[...].astype(F32)
    inverse = lax.rsqrt(jnp.mean(value * value, axis=-1, keepdims=True) + EPS)
    rinv[...] = jnp.broadcast_to(inverse, rinv.shape)
    width = acts.shape[1] // X
    span = width // (Z * C)
    for step in range(X):
        base = lax.rem(place[0] + step, X) * width
        for number in range(Z * C):
            core, flip = number // Z, number % Z
            local = (place[1] ^ flip) * (C * span) + (place[2] ^ core) * span
            lanes = pl.ds(pl.multiple_of(base + local, span), span)
            part = acts[:, lanes].astype(F32) * inverse
            slots[step][:, number * span : (number + 1) * span] = (part * gain[:, lanes]).astype(BF16)
        slots[step][:, width:] = cot[...]


def normalise(place, acts, gain, cot):
    tokens, width = acts.shape
    keys = cot.shape[1]
    rows = 64
    part = width // X + keys
    whole = lambda i, place: (0, 0)
    return pl.pallas_call(
        norm_kernel,
        grid_spec=pltpu.PrefetchScalarGridSpec(
            num_scalar_prefetch=1,
            grid=(tokens // rows,),
            in_specs=[
                pl.BlockSpec((rows, width), lambda i, place: (i, 0)),
                pl.BlockSpec((1, width), whole),
                pl.BlockSpec((rows, keys), lambda i, place: (i, 0)),
            ],
            out_specs=[pl.BlockSpec((rows, 128), lambda i, place: (i, 0))]
            + [pl.BlockSpec((rows, part), lambda i, place: (i, 0))] * X,
        ),
        out_shape=[jax.ShapeDtypeStruct((tokens, 128), F32)]
        + [jax.ShapeDtypeStruct((tokens, part), BF16)] * X,
        compiler_params=params(),
        name="normalise",
    )(place, acts, gain, cot)


def pack_kernel(
    r0, r1, r2, r3, second, third, hold, features, rest, base, wide, blocks, early, arrive, leave
):
    tokens = r0.shape[0]
    skip = r0.shape[1] - features.shape[1]
    span = second.shape[0]
    moves = [
        (second, blocks.at[pl.ds(0, span)], rest.at[pl.ds(0, span)]),
        (third, blocks.at[pl.ds(span, third.shape[0])], rest.at[pl.ds(span, third.shape[0])]),
    ]
    moves.append((hold, early, base.at[pl.ds(0, hold.shape[0])]))
    for number, r in enumerate((r0, r1, r2, r3)):
        part = pl.ds(number * tokens, tokens)
        moves.append((r.at[:, pl.ds(skip, features.shape[1])], wide.at[part], features.at[part]))
    loads = [pltpu.make_async_copy(m[0], m[1], arrive.at[i]) for i, m in enumerate(moves)]
    stores = [pltpu.make_async_copy(m[1], m[2], leave.at[i]) for i, m in enumerate(moves)]
    again = pltpu.make_async_copy(
        moves[1][1], base.at[pl.ds(hold.shape[0], third.shape[0])], leave.at[len(moves)]
    )
    for load in loads:
        load.start()
    for load, store in zip(loads, stores):
        load.wait()
        store.start()
    again.start()
    for store in stores + [again]:
        store.wait()


def pack(rows, second, third, hold, span):
    tokens, width = rows[0].shape
    hbm = pl.BlockSpec(memory_space=pl.ANY)
    shapes = [
        (X * tokens, width - Z * span),
        (second.shape[0] + third.shape[0], second.shape[1]),
        (hold.shape[0] + third.shape[0], second.shape[1]),
    ]
    return pl.pallas_call(
        pack_kernel,
        in_specs=[hbm] * (X + 3),
        out_specs=[hbm] * 3,
        out_shape=[jax.ShapeDtypeStruct(shape, BF16) for shape in shapes],
        scratch_shapes=[pltpu.VMEM(shape, BF16) for shape in (*shapes[:2], hold.shape)]
        + [pltpu.SemaphoreType.DMA((X + 3,)), pltpu.SemaphoreType.DMA((X + 4,))],
        compiler_params=params(),
        name="pack",
    )(*rows, second, third, hold)


def wgrad_kernel(r0, r1, r2, r3, other, kept, sent1, sent3):
    span = kept.shape[1]
    own, width = Z * span, Z * C * span
    mine = (r0, r1, r2, r3)
    cots = jnp.concatenate([r[:, width:] for r in mine] + [other[:, own:]], axis=0)
    for flip in range(Z):
        lanes = slice(flip * span, (flip + 1) * span)
        rows = jnp.concatenate([r[:, lanes] for r in mine] + [other[:, lanes]], axis=0)
        total = lax.dot_general(
            rows, cots, (((0,), (0,)), ((), ())), preferred_element_type=F32
        )
        if flip % 2:
            (sent3 if flip == 3 else sent1)[...] = total.astype(BF16)
        else:
            kept[flip // 2] = total


def wgrad_part(rows, other, span, keys):
    vmem = pl.BlockSpec(memory_space=pltpu.VMEM)
    return pl.pallas_call(
        wgrad_kernel,
        in_specs=[vmem] * (X + 1),
        out_specs=[vmem] * 3,
        out_shape=[
            jax.ShapeDtypeStruct((2, span, keys), F32),
            jax.ShapeDtypeStruct((span, keys), BF16),
            jax.ShapeDtypeStruct((span, keys), BF16),
        ],
        compiler_params=params(),
        name="wgrad_part",
    )(*rows, other)


def pieces_of(layout, refs, place, part):
    span = part // (Z * C)
    pieces = []
    for slot, flips, *sources in layout:
        block = lax.rem(place[0] + OFFSETS[slot], X)
        for source, which in zip(sources, (place[2], 1 - place[2])):
            if source is None:
                continue
            number, first = source
            for row, flip in enumerate(flips, first):
                local = pl.multiple_of((place[1] ^ flip) * (C * span) + which * span, span)
                start = pl.multiple_of(block * part + local, span)
                rows = slice(row * span, (row + 1) * span)
                pieces.append((slot, start, local, refs[number], rows))
    return pieces


def keys_sum(pieces, acts, gain, inverse):
    total = None
    for _, start, _, ref, rows in pieces:
        lanes = pl.ds(start, rows.stop - rows.start)
        hat = acts[:, lanes].astype(F32) * inverse
        normed = (hat * gain[:, lanes]).astype(BF16)
        term = jnp.dot(normed, ref[rows, :], preferred_element_type=F32)
        total = term if total is None else total + term
    return total


def cotangent_of(cots, ref, rows):
    return lax.dot_general(
        cots, ref[rows, :], (((1,), (1,)), ((), ())), preferred_element_type=F32
    )


def early_kernel(layout, started, hold, place, acts, gain, rinv, cot, *refs):
    weights, (keys, scaled) = refs[started : -2 - hold], refs[-2 - hold :][:2]
    if hold:
        span = weights[0].shape[0]
        for number, ref in enumerate(weights):
            refs[-1][number * span : (number + 1) * span, :] = ref[...]
    part = acts.shape[1] // X
    inverse = rinv[:, :1]
    pieces = pieces_of(layout, weights, place, part)
    total = keys_sum(pieces, acts, gain, inverse)
    keys[...] = refs[0][...] + total if started else total
    cots = cot[...]
    for number, (_, start, _, ref, rows) in enumerate(pieces):
        span = rows.stop - rows.start
        scaled[number] = inverse * cotangent_of(cots, ref, rows) * gain[:, pl.ds(start, span)]


def backward_early(place, acts, gain, rinv, cot, before, layout, weights, hold=0):
    tokens, width = acts.shape
    span = width // (X * Z * C)
    pieces = sum(len(flips) * (2 - sources.count(None)) for _, flips, *sources in layout)
    vmem = pl.BlockSpec(memory_space=pltpu.VMEM)
    return pl.pallas_call(
        functools.partial(early_kernel, layout, len(before), hold),
        in_specs=[pl.BlockSpec(memory_space=pltpu.SMEM)]
        + [vmem] * (4 + len(before) + len(weights)),
        out_specs=[vmem] * (2 + hold),
        out_shape=[
            jax.ShapeDtypeStruct((tokens, cot.shape[1]), F32),
            jax.ShapeDtypeStruct((pieces, tokens, span), F32),
        ]
        + [jax.ShapeDtypeStruct((len(weights) * span, cot.shape[1]), BF16)] * hold,
        compiler_params=params(),
        name="backward_early",
    )(place, acts, gain, rinv, cot, *before, *weights)


def late_kernel(layout, done, place, acts, gain, rinv, cot, early, *refs):
    sources, refs = refs[: len(done)], refs[len(done) :]
    weights, (keys, dx, held, leave) = refs[:-4], refs[-4:]
    tokens, width = acts.shape
    part = width // X
    inverse = rinv[:, :1]
    pieces = pieces_of(layout, weights, place, part)
    total = early[...] + keys_sum(pieces, acts, gain, inverse)
    keys[...] = total
    cots = cot[...]
    inner = jnp.sum(total * cots.astype(F32), axis=-1, keepdims=True) / width
    factor = rinv[...] * rinv[...] * jnp.broadcast_to(inner, rinv.shape)
    lane = factor.shape[1]
    copies = []

    def send(slot):
        start = pl.multiple_of(lax.rem(place[0] + OFFSETS[slot], X) * part, part)
        lanes = pl.ds(start, part)
        copy = pltpu.make_async_copy(held.at[:, lanes], dx.at[:, lanes], leave.at[slot])
        copy.start()
        copies.append(copy)

    for slot in range(X - 1):
        for source, entries in zip(sources, done):
            for number, (at, start, _, _, rows) in enumerate(
                pieces_of(entries, [None] * 16, place, part)
            ):
                if at != slot:
                    continue
                for first in range(0, rows.stop - rows.start, lane):
                    lanes = pl.ds(pl.multiple_of(start + first, lane), lane)
                    held[:, lanes] = (
                        source[number, :, first : first + lane]
                        - acts[:, lanes].astype(F32) * factor
                    )
        send(slot)
    for slot, start, _, ref, rows in pieces:
        cotangent = cotangent_of(cots, ref, rows)
        for first in range(0, rows.stop - rows.start, lane):
            lanes = pl.ds(pl.multiple_of(start + first, lane), lane)
            held[:, lanes] = (
                rinv[...] * cotangent[:, first : first + lane] * gain[:, lanes]
                - acts[:, lanes].astype(F32) * factor
            )
    send(X - 1)
    for copy in copies:
        copy.wait()


def backward_late(place, acts, gain, rinv, cot, early, sources, done, layout, weights):
    tokens, width = acts.shape
    vmem = pl.BlockSpec(memory_space=pltpu.VMEM)
    return pl.pallas_call(
        functools.partial(late_kernel, layout, done),
        in_specs=[pl.BlockSpec(memory_space=pltpu.SMEM)]
        + [vmem] * (5 + len(sources) + len(weights)),
        out_specs=[vmem, pl.BlockSpec(memory_space=pl.ANY)],
        out_shape=[
            jax.ShapeDtypeStruct((tokens, cot.shape[1]), F32),
            jax.ShapeDtypeStruct((tokens, width), F32),
        ],
        scratch_shapes=[pltpu.VMEM((tokens, width), F32), pltpu.SemaphoreType.DMA((X,))],
        compiler_params=params(),
        name="backward_late",
    )(place, acts, gain, rinv, cot, early, *sources, *weights)


def delta_kernel(place, glob, local, out):
    out[...] = glob[...] - local[...]


def delta(place, glob, local, first, stride):
    rows, width = glob.shape
    block = (1, rows // Y, width)
    theirs = pl.BlockSpec(block, lambda i, place: (place[3] ^ (first + stride * i), 0, 0))
    parts = (Y, rows // Y, width)
    return pl.pallas_call(
        delta_kernel,
        grid_spec=pltpu.PrefetchScalarGridSpec(
            num_scalar_prefetch=1,
            grid=(2,),
            in_specs=[theirs, theirs],
            out_specs=pl.BlockSpec(block, lambda i, place: (i, 0, 0)),
        ),
        out_shape=jax.ShapeDtypeStruct((2, rows // Y, width), F32),
        compiler_params=params(),
        name="delta",
    )(place, glob.reshape(parts), local.reshape(parts))


def outer_kernel(place, p03, p12, glob, codes, scales, new_global, new_codes, new_scales):
    rows = p03.shape[1]
    blocks = scales.shape[0]
    span = p03.shape[2] // blocks
    columns = jnp.concatenate([scales[...]] * (128 // blocks), axis=0).T
    spread = 128 // blocks
    for flip, part in ((0, p03.at[0]), (3, p03.at[1]), (1, p12.at[0]), (2, p12.at[1])):
        start = pl.multiple_of((place[3] ^ flip) * rows, rows)
        new_global[pl.ds(start, rows), :] = part[...]
    maxima = []
    for block in range(blocks):
        lanes = slice(block * span, (block + 1) * span)
        pseudo = new_global[:, lanes]
        momentum = codes[:, lanes].astype(F32) * columns[:, block : block + 1]
        moved = MU * momentum + pseudo
        new_global[:, lanes] = glob[:, lanes] - RATE * (pseudo + MU * moved)
        scale = jnp.max(jnp.abs(moved), axis=-1, keepdims=True) + 1e-06
        new_codes[:, lanes] = (moved / scale).astype(BF16)
        maxima.append(jnp.broadcast_to(scale, (Y * rows, spread)))
    across = jnp.concatenate(maxima, axis=-1).T
    new_scales[...] = jnp.concatenate(
        [across[start : start + 1] for start in range(0, 128, spread)], axis=0
    )


def outer_update(place, p03, p12, glob, codes, scales):
    vmem = pl.BlockSpec(memory_space=pltpu.VMEM)
    new_global, new_codes, new_scales = pl.pallas_call(
        outer_kernel,
        in_specs=[pl.BlockSpec(memory_space=pltpu.SMEM)] + [vmem] * 5,
        out_specs=[vmem] * 3,
        out_shape=[
            jax.ShapeDtypeStruct(glob.shape, F32),
            jax.ShapeDtypeStruct(codes.shape, BF16),
            jax.ShapeDtypeStruct(scales.shape[::-1], F32),
        ],
        compiler_params=params(),
        name="outer_update",
    )(place, p03, p12, glob, codes, scales.T)
    return new_global, new_codes, new_scales.T


def together(*values):
    return lax.optimization_barrier(values)


def body(
    activations,
    norm_gain,
    key_weight,
    key_cotangent,
    local_fragment,
    global_fragment,
    momentum_codes,
    momentum_scales,
):
    acts, weight, cot = activations[0], key_weight[0], key_cotangent[0]
    here, replica = lax.axis_index("fsdp"), lax.axis_index("replica")
    place = jnp.stack([here // (Z * C), (here // C) % Z, here % C, replica // H]).astype(jnp.int32)
    span = weight.shape[0]

    width = cot.shape[1]
    second = shift(weight, flip=1)
    near3, near1 = shift(weight, dx=1), shift(weight, dx=-1)
    came = trade(delta(place, global_fragment, local_fragment[0], 1, 1), flip=1)
    rinv, *slots = normalise(place, acts, norm_gain, cot)
    *slots, second, near3, near1, came, glob = together(
        *slots, second, near3, near1, came, global_fragment
    )

    rows = [slots[0]] + [shift(slots[d], dx=d) for d in (1, 3, 2)]
    third = shift(jnp.concatenate([weight, second], axis=0), flip=2)
    quarter = global_fragment.shape[0] // Y
    own_delta = [
        lax.dynamic_slice_in_dim(glob, (place[3] ^ flip) * quarter, quarter)
        - lax.dynamic_slice_in_dim(local_fragment[0], (place[3] ^ flip) * quarter, quarter)
        for flip in (0, 3)
    ]
    total = own_delta[0] + came[0] + trade(own_delta[1] + came[1], flip=3)
    came = trade(total, far=1)
    early, first, hold = backward_early(
        place, acts, norm_gain, rinv, cot, (), FIRST, (weight, second, near1, near3), hold=1
    )
    *rows, third, came, early = together(*rows, third, came, early)
    pseudo = (total + came) / (Y * H)

    other, rest, base = pack(rows, second, third, hold, span)
    other = shift(other, swap=1)
    far3, far1 = shift(rest, dx=1), shift(rest, dx=-1)
    came = trade(pseudo, flip=3)
    other, came = together(other, came)
    p03 = jnp.stack([pseudo, came])
    p12 = trade(p03, flip=1)
    kept, sent1, sent3 = wgrad_part(rows, other, span, width)
    base_mate = shift(base, swap=1)
    early, sent1 = together(early, sent1)
    early, second_part = backward_early(
        place, acts, norm_gain, rinv, cot, (early,), SECOND, (third, base_mate)
    )
    back3 = shift(sent3, flip=1)
    far3, far1, early, back3, p12 = together(far3, far1, early, back3, p12)

    across_a = shift(jnp.concatenate([near1, far1[:span]], axis=0), dx=-1)
    across_b = shift(far3[span:], dx=1)
    far = jnp.concatenate([far1, far3], axis=0)
    far_mate = shift(far, swap=1)
    last = (kept[1] + back3.astype(F32)).astype(BF16)
    end = shift(last, flip=2)
    back1 = shift(sent1, flip=1)
    early, third_part = backward_early(
        place, acts, norm_gain, rinv, cot, (early,), THIRD, (far, far_mate)
    )
    new_global, new_codes, new_scales = outer_update(
        place, p03, p12, global_fragment, momentum_codes, momentum_scales
    )
    across_a, across_b, early, new_scales, end, back1 = together(
        across_a, across_b, early, new_scales, end, back1
    )
    mate_a, mate_b = shift(across_a, swap=1), shift(across_b, swap=1)
    weight_grad = kept[0] + back1.astype(F32) + end.astype(F32)
    gain_here = lax.dynamic_slice_in_dim(norm_gain[0], here * span, span)
    gain_grad = jnp.sum(weight.astype(F32) * weight_grad, axis=-1) / gain_here
    mate_a, mate_b, gain_grad = together(mate_a, mate_b, gain_grad)
    keys, input_gradient_rows = backward_late(
        place, acts, norm_gain, rinv, cot, early, (first, second_part, third_part),
        (FIRST, SECOND, THIRD), LAST, (across_a, mate_a, across_b, mate_b),
    )
    return (
        keys[None],
        weight_grad[None],
        gain_grad[None],
        input_gradient_rows[None],
        new_global,
        new_codes,
        new_scales,
    )


def solution(mesh):
    in_specs = (
        P("replica", "fsdp", None),
        P("replica", None),
        P("replica", "fsdp", None),
        P("replica", "fsdp", None),
        P("replica", "fsdp", None),
        P("fsdp", None),
        P("fsdp", None),
        P("fsdp", None),
    )
    out_specs = (
        P("replica", "fsdp", None),
        P("replica", "fsdp", None),
        P("replica", "fsdp"),
        P("replica", "fsdp", None),
        P("fsdp", None),
        P("fsdp", None),
        P("fsdp", None),
    )
    return jax.shard_map(body, mesh=mesh, in_specs=in_specs, out_specs=out_specs, check_vma=False)
```

```python
import functools

import jax
import jax.numpy as jnp
from jax import lax
from jax.experimental import pallas as pl
from jax.experimental.pallas import tpu as pltpu
from jax.sharding import PartitionSpec as P

EPS = 1e-05
MU = 0.9
RATE = 0.7
X, Z, C = 4, 4, 2
Y, H = 4, 2
OFFSETS = (0, 1, 3, 2)
FIRST = (
    (0, (0,), (0, 0), None),
    (0, (1,), (1, 0), None),
    (1, (0,), (2, 0), None),
    (2, (0,), (3, 0), None),
)
SECOND = (
    (0, (2, 3), (0, 0), (1, 4)),
    (0, (0, 1), None, (1, 0)),
    (1, (0,), None, (1, 2)),
    (2, (0,), None, (1, 3)),
)
THIRD = ((1, (1, 2, 3), (0, 0), (1, 0)), (2, (1, 2, 3), (0, 3), (1, 3)))
LAST = ((3, (0, 1), (0, 0), (1, 0)), (3, (2, 3), (2, 0), (3, 0)))
VMEM_LIMIT = 56 * 1024 * 1024
F32 = jnp.float32
BF16 = jnp.bfloat16


def index_of(x, z, c):
    return (x * Z + z) * C + c


def shift(value, dx=0, flip=0, swap=0):
    moves = [
        (index_of(x, z, c), index_of((x + dx) % X, z ^ flip, c ^ swap))
        for x in range(X)
        for z in range(Z)
        for c in range(C)
    ]
    return lax.ppermute(value, "fsdp", moves)


def trade(value, flip=0, far=0):
    moves = [(y * H + h, (y ^ flip) * H + (h ^ far)) for y in range(Y) for h in range(H)]
    return lax.ppermute(value, "replica", moves)


def params(**kw):
    return pltpu.CompilerParams(vmem_limit_bytes=VMEM_LIMIT, **kw)


def norm_kernel(place, acts, gain, cot, rinv, *slots):
    value = acts[...].astype(F32)
    inverse = lax.rsqrt(jnp.mean(value * value, axis=-1, keepdims=True) + EPS)
    rinv[...] = jnp.broadcast_to(inverse, rinv.shape)
    width = acts.shape[1] // X
    span = width // (Z * C)
    for step in range(X):
        base = lax.rem(place[0] + step, X) * width
        for number in range(Z * C):
            core, flip = number // Z, number % Z
            local = (place[1] ^ flip) * (C * span) + (place[2] ^ core) * span
            lanes = pl.ds(pl.multiple_of(base + local, span), span)
            part = acts[:, lanes].astype(F32) * inverse
            slots[step][:, number * span : (number + 1) * span] = (part * gain[:, lanes]).astype(BF16)
        slots[step][:, width:] = cot[...]


def normalise(place, acts, gain, cot):
    tokens, width = acts.shape
    keys = cot.shape[1]
    rows = 64
    part = width // X + keys
    whole = lambda i, place: (0, 0)
    return pl.pallas_call(
        norm_kernel,
        grid_spec=pltpu.PrefetchScalarGridSpec(
            num_scalar_prefetch=1,
            grid=(tokens // rows,),
            in_specs=[
                pl.BlockSpec((rows, width), lambda i, place: (i, 0)),
                pl.BlockSpec((1, width), whole),
                pl.BlockSpec((rows, keys), lambda i, place: (i, 0)),
            ],
            out_specs=[pl.BlockSpec((rows, 128), lambda i, place: (i, 0))]
            + [pl.BlockSpec((rows, part), lambda i, place: (i, 0))] * X,
        ),
        out_shape=[jax.ShapeDtypeStruct((tokens, 128), F32)]
        + [jax.ShapeDtypeStruct((tokens, part), BF16)] * X,
        compiler_params=params(),
        name="normalise",
    )(place, acts, gain, cot)


def pack_kernel(
    r0, r1, r2, r3, second, third, hold, features, rest, base, wide, blocks, early, arrive, leave
):
    tokens = r0.shape[0]
    skip = r0.shape[1] - features.shape[1]
    span = second.shape[0]
    moves = [
        (second, blocks.at[pl.ds(0, span)], rest.at[pl.ds(0, span)]),
        (third, blocks.at[pl.ds(span, third.shape[0])], rest.at[pl.ds(span, third.shape[0])]),
    ]
    moves.append((hold, early, base.at[pl.ds(0, hold.shape[0])]))
    for number, r in enumerate((r0, r1, r2, r3)):
        part = pl.ds(number * tokens, tokens)
        moves.append((r.at[:, pl.ds(skip, features.shape[1])], wide.at[part], features.at[part]))
    loads = [pltpu.make_async_copy(m[0], m[1], arrive.at[i]) for i, m in enumerate(moves)]
    stores = [pltpu.make_async_copy(m[1], m[2], leave.at[i]) for i, m in enumerate(moves)]
    again = pltpu.make_async_copy(
        moves[1][1], base.at[pl.ds(hold.shape[0], third.shape[0])], leave.at[len(moves)]
    )
    for load in loads:
        load.start()
    for load, store in zip(loads, stores):
        load.wait()
        store.start()
    again.start()
    for store in stores + [again]:
        store.wait()


def pack(rows, second, third, hold, span):
    tokens, width = rows[0].shape
    hbm = pl.BlockSpec(memory_space=pl.ANY)
    shapes = [
        (X * tokens, width - Z * span),
        (second.shape[0] + third.shape[0], second.shape[1]),
        (hold.shape[0] + third.shape[0], second.shape[1]),
    ]
    return pl.pallas_call(
        pack_kernel,
        in_specs=[hbm] * (X + 3),
        out_specs=[hbm] * 3,
        out_shape=[jax.ShapeDtypeStruct(shape, BF16) for shape in shapes],
        scratch_shapes=[pltpu.VMEM(shape, BF16) for shape in (*shapes[:2], hold.shape)]
        + [pltpu.SemaphoreType.DMA((X + 3,)), pltpu.SemaphoreType.DMA((X + 4,))],
        compiler_params=params(),
        name="pack",
    )(*rows, second, third, hold)


def wgrad_kernel(r0, r1, r2, r3, other, kept, sent1, sent3):
    span = kept.shape[1]
    own, width = Z * span, Z * C * span
    mine = (r0, r1, r2, r3)
    cots = jnp.concatenate([r[:, width:] for r in mine] + [other[:, own:]], axis=0)
    for flip in range(Z):
        lanes = slice(flip * span, (flip + 1) * span)
        rows = jnp.concatenate([r[:, lanes] for r in mine] + [other[:, lanes]], axis=0)
        total = lax.dot_general(
            rows, cots, (((0,), (0,)), ((), ())), preferred_element_type=F32
        )
        if flip % 2:
            (sent3 if flip == 3 else sent1)[...] = total.astype(BF16)
        else:
            kept[flip // 2] = total


def wgrad_part(rows, other, span, keys):
    vmem = pl.BlockSpec(memory_space=pltpu.VMEM)
    return pl.pallas_call(
        wgrad_kernel,
        in_specs=[vmem] * (X + 1),
        out_specs=[vmem] * 3,
        out_shape=[
            jax.ShapeDtypeStruct((2, span, keys), F32),
            jax.ShapeDtypeStruct((span, keys), BF16),
            jax.ShapeDtypeStruct((span, keys), BF16),
        ],
        compiler_params=params(),
        name="wgrad_part",
    )(*rows, other)


def pieces_of(layout, refs, place, part):
    span = part // (Z * C)
    pieces = []
    for slot, flips, *sources in layout:
        block = lax.rem(place[0] + OFFSETS[slot], X)
        for source, which in zip(sources, (place[2], 1 - place[2])):
            if source is None:
                continue
            number, first = source
            for row, flip in enumerate(flips, first):
                local = pl.multiple_of((place[1] ^ flip) * (C * span) + which * span, span)
                start = pl.multiple_of(block * part + local, span)
                rows = slice(row * span, (row + 1) * span)
                pieces.append((slot, start, local, refs[number], rows))
    return pieces


def keys_sum(pieces, acts, gain, inverse):
    total = None
    for _, start, _, ref, rows in pieces:
        lanes = pl.ds(start, rows.stop - rows.start)
        hat = acts[:, lanes].astype(F32) * inverse
        normed = (hat * gain[:, lanes]).astype(BF16)
        term = jnp.dot(normed, ref[rows, :], preferred_element_type=F32)
        total = term if total is None else total + term
    return total


def cotangent_of(cots, ref, rows):
    return lax.dot_general(
        cots, ref[rows, :], (((1,), (1,)), ((), ())), preferred_element_type=F32
    )


def early_kernel(layout, started, hold, place, acts, gain, rinv, cot, *refs):
    weights, (keys, scaled) = refs[started : -2 - hold], refs[-2 - hold :][:2]
    if hold:
        span = weights[0].shape[0]
        for number, ref in enumerate(weights):
            refs[-1][number * span : (number + 1) * span, :] = ref[...]
    part = acts.shape[1] // X
    inverse = rinv[:, :1]
    pieces = pieces_of(layout, weights, place, part)
    total = keys_sum(pieces, acts, gain, inverse)
    keys[...] = refs[0][...] + total if started else total
    cots = cot[...]
    for number, (_, start, _, ref, rows) in enumerate(pieces):
        span = rows.stop - rows.start
        scaled[number] = inverse * cotangent_of(cots, ref, rows) * gain[:, pl.ds(start, span)]


def backward_early(place, acts, gain, rinv, cot, before, layout, weights, hold=0):
    tokens, width = acts.shape
    span = width // (X * Z * C)
    pieces = sum(len(flips) * (2 - sources.count(None)) for _, flips, *sources in layout)
    vmem = pl.BlockSpec(memory_space=pltpu.VMEM)
    return pl.pallas_call(
        functools.partial(early_kernel, layout, len(before), hold),
        in_specs=[pl.BlockSpec(memory_space=pltpu.SMEM)]
        + [vmem] * (4 + len(before) + len(weights)),
        out_specs=[vmem] * (2 + hold),
        out_shape=[
            jax.ShapeDtypeStruct((tokens, cot.shape[1]), F32),
            jax.ShapeDtypeStruct((pieces, tokens, span), F32),
        ]
        + [jax.ShapeDtypeStruct((len(weights) * span, cot.shape[1]), BF16)] * hold,
        compiler_params=params(),
        name="backward_early",
    )(place, acts, gain, rinv, cot, *before, *weights)


def late_kernel(layout, done, place, acts, gain, rinv, cot, early, *refs):
    sources, refs = refs[: len(done)], refs[len(done) :]
    weights, (keys, dx, held, leave) = refs[:-4], refs[-4:]
    tokens, width = acts.shape
    part = width // X
    inverse = rinv[:, :1]
    pieces = pieces_of(layout, weights, place, part)
    total = early[...] + keys_sum(pieces, acts, gain, inverse)
    keys[...] = total
    cots = cot[...]
    inner = jnp.sum(total * cots.astype(F32), axis=-1, keepdims=True) / width
    factor = rinv[...] * rinv[...] * jnp.broadcast_to(inner, rinv.shape)
    lane = factor.shape[1]
    copies = []

    def send(slot):
        start = pl.multiple_of(lax.rem(place[0] + OFFSETS[slot], X) * part, part)
        lanes = pl.ds(start, part)
        copy = pltpu.make_async_copy(held.at[:, lanes], dx.at[:, lanes], leave.at[slot])
        copy.start()
        copies.append(copy)

    for slot in range(X - 1):
        for source, entries in zip(sources, done):
            for number, (at, start, _, _, rows) in enumerate(
                pieces_of(entries, [None] * 16, place, part)
            ):
                if at != slot:
                    continue
                for first in range(0, rows.stop - rows.start, lane):
                    lanes = pl.ds(pl.multiple_of(start + first, lane), lane)
                    held[:, lanes] = (
                        source[number, :, first : first + lane]
                        - acts[:, lanes].astype(F32) * factor
                    )
        send(slot)
    for slot, start, _, ref, rows in pieces:
        cotangent = cotangent_of(cots, ref, rows)
        for first in range(0, rows.stop - rows.start, lane):
            lanes = pl.ds(pl.multiple_of(start + first, lane), lane)
            held[:, lanes] = (
                rinv[...] * cotangent[:, first : first + lane] * gain[:, lanes]
                - acts[:, lanes].astype(F32) * factor
            )
    send(X - 1)
    for copy in copies:
        copy.wait()


def backward_late(place, acts, gain, rinv, cot, early, sources, done, layout, weights):
    tokens, width = acts.shape
    vmem = pl.BlockSpec(memory_space=pltpu.VMEM)
    return pl.pallas_call(
        functools.partial(late_kernel, layout, done),
        in_specs=[pl.BlockSpec(memory_space=pltpu.SMEM)]
        + [vmem] * (5 + len(sources) + len(weights)),
        out_specs=[vmem, pl.BlockSpec(memory_space=pl.ANY)],
        out_shape=[
            jax.ShapeDtypeStruct((tokens, cot.shape[1]), F32),
            jax.ShapeDtypeStruct((tokens, width), F32),
        ],
        scratch_shapes=[pltpu.VMEM((tokens, width), F32), pltpu.SemaphoreType.DMA((X,))],
        compiler_params=params(),
        name="backward_late",
    )(place, acts, gain, rinv, cot, early, *sources, *weights)


def delta_kernel(place, glob, local, keep, send):
    rows = keep.shape[1]
    for flip, out, row in ((0, keep, 0), (3, keep, 1), (1, send, 0), (2, send, 1)):
        part = pl.ds(pl.multiple_of((place[3] ^ flip) * rows, rows), rows)
        out[row] = glob[part, :] - local[part, :]


def delta(place, glob, local):
    rows, width = glob.shape
    vmem = pl.BlockSpec(memory_space=pltpu.VMEM)
    return pl.pallas_call(
        delta_kernel,
        in_specs=[pl.BlockSpec(memory_space=pltpu.SMEM), vmem, vmem],
        out_specs=[vmem, vmem],
        out_shape=[jax.ShapeDtypeStruct((2, rows // Y, width), F32)] * 2,
        compiler_params=params(),
        name="delta",
    )(place, glob, local)


def outer_kernel(place, p03, p12, glob, codes, scales, new_global, new_codes, new_scales):
    rows = p03.shape[1]
    blocks = scales.shape[0]
    span = p03.shape[2] // blocks
    columns = jnp.concatenate([scales[...]] * (128 // blocks), axis=0).T
    spread = 128 // blocks
    for flip, part in ((0, p03.at[0]), (3, p03.at[1]), (1, p12.at[0]), (2, p12.at[1])):
        start = pl.multiple_of((place[3] ^ flip) * rows, rows)
        new_global[pl.ds(start, rows), :] = part[...]
    maxima = []
    for block in range(blocks):
        lanes = slice(block * span, (block + 1) * span)
        pseudo = new_global[:, lanes]
        momentum = codes[:, lanes].astype(F32) * columns[:, block : block + 1]
        moved = MU * momentum + pseudo
        new_global[:, lanes] = glob[:, lanes] - RATE * (pseudo + MU * moved)
        scale = jnp.max(jnp.abs(moved), axis=-1, keepdims=True) + 1e-06
        new_codes[:, lanes] = (moved / scale).astype(BF16)
        maxima.append(jnp.broadcast_to(scale, (Y * rows, spread)))
    across = jnp.concatenate(maxima, axis=-1).T
    new_scales[...] = jnp.concatenate(
        [across[start : start + 1] for start in range(0, 128, spread)], axis=0
    )


def outer_update(place, p03, p12, glob, codes, scales):
    vmem = pl.BlockSpec(memory_space=pltpu.VMEM)
    new_global, new_codes, new_scales = pl.pallas_call(
        outer_kernel,
        in_specs=[pl.BlockSpec(memory_space=pltpu.SMEM)] + [vmem] * 5,
        out_specs=[vmem] * 3,
        out_shape=[
            jax.ShapeDtypeStruct(glob.shape, F32),
            jax.ShapeDtypeStruct(codes.shape, BF16),
            jax.ShapeDtypeStruct(scales.shape[::-1], F32),
        ],
        compiler_params=params(),
        name="outer_update",
    )(place, p03, p12, glob, codes, scales.T)
    return new_global, new_codes, new_scales.T


def together(*values):
    return lax.optimization_barrier(values)


def body(
    activations,
    norm_gain,
    key_weight,
    key_cotangent,
    local_fragment,
    global_fragment,
    momentum_codes,
    momentum_scales,
):
    acts, weight, cot = activations[0], key_weight[0], key_cotangent[0]
    here, replica = lax.axis_index("fsdp"), lax.axis_index("replica")
    place = jnp.stack([here // (Z * C), (here // C) % Z, here % C, replica // H]).astype(jnp.int32)
    span = weight.shape[0]

    width = cot.shape[1]
    second = shift(weight, flip=1)
    near3, near1 = shift(weight, dx=1), shift(weight, dx=-1)
    keep, send = delta(place, global_fragment, local_fragment[0])
    came = trade(send, flip=1)
    rinv, *slots = normalise(place, acts, norm_gain, cot)
    *slots, second, near3, near1, came = together(*slots, second, near3, near1, came)

    rows = [slots[0]] + [shift(slots[d], dx=d) for d in (1, 3, 2)]
    third = shift(jnp.concatenate([weight, second], axis=0), flip=2)
    keep = keep + came
    total = keep[0] + trade(keep[1], flip=3)
    came = trade(total, far=1)
    early, first, hold = backward_early(
        place, acts, norm_gain, rinv, cot, (), FIRST, (weight, second, near1, near3), hold=1
    )
    *rows, third, came, early = together(*rows, third, came, early)
    pseudo = (total + came) / (Y * H)

    other, rest, base = pack(rows, second, third, hold, span)
    other = shift(other, swap=1)
    far3, far1 = shift(rest, dx=1), shift(rest, dx=-1)
    came = trade(pseudo, flip=3)
    other, came = together(other, came)
    p03 = jnp.stack([pseudo, came])
    p12 = trade(p03, flip=1)
    kept, sent1, sent3 = wgrad_part(rows, other, span, width)
    base_mate = shift(base, swap=1)
    early, sent1 = together(early, sent1)
    early, second_part = backward_early(
        place, acts, norm_gain, rinv, cot, (early,), SECOND, (third, base_mate)
    )
    back3 = shift(sent3, flip=1)
    far3, far1, early, back3, p12 = together(far3, far1, early, back3, p12)

    across_a = shift(jnp.concatenate([near1, far1[:span]], axis=0), dx=-1)
    across_b = shift(far3[span:], dx=1)
    far = jnp.concatenate([far1, far3], axis=0)
    far_mate = shift(far, swap=1)
    last = (kept[1] + back3.astype(F32)).astype(BF16)
    end = shift(last, flip=2)
    back1 = shift(sent1, flip=1)
    early, third_part = backward_early(
        place, acts, norm_gain, rinv, cot, (early,), THIRD, (far, far_mate)
    )
    early, end, back1 = together(early, end, back1)
    weight_grad = kept[0] + back1.astype(F32) + end.astype(F32)
    gain_here = lax.dynamic_slice_in_dim(norm_gain[0], here * span, span)
    gain_grad = jnp.sum(weight.astype(F32) * weight_grad, axis=-1) / gain_here
    new_global, new_codes, new_scales = outer_update(
        place, p03, p12, global_fragment, momentum_codes, momentum_scales
    )
    across_a, across_b, early, gain_grad, new_scales = together(
        across_a, across_b, early, gain_grad, new_scales
    )
    mate_a, mate_b = shift(across_a, swap=1), shift(across_b, swap=1)
    keys, input_gradient_rows = backward_late(
        place, acts, norm_gain, rinv, cot, early, (first, second_part, third_part),
        (FIRST, SECOND, THIRD), LAST, (across_a, mate_a, across_b, mate_b),
    )
    return (
        keys[None],
        weight_grad[None],
        gain_grad[None],
        input_gradient_rows[None],
        new_global,
        new_codes,
        new_scales,
    )


def solution(mesh):
    in_specs = (
        P("replica", "fsdp", None),
        P("replica", None),
        P("replica", "fsdp", None),
        P("replica", "fsdp", None),
        P("replica", "fsdp", None),
        P("fsdp", None),
        P("fsdp", None),
        P("fsdp", None),
    )
    out_specs = (
        P("replica", "fsdp", None),
        P("replica", "fsdp", None),
        P("replica", "fsdp"),
        P("replica", "fsdp", None),
        P("fsdp", None),
        P("fsdp", None),
        P("fsdp", None),
    )
    return jax.shard_map(body, mesh=mesh, in_specs=in_specs, out_specs=out_specs, check_vma=False)
```

```python
import functools

import jax
import jax.numpy as jnp
from jax import lax
from jax.experimental import pallas as pl
from jax.experimental.pallas import tpu as pltpu
from jax.sharding import PartitionSpec as P

EPS = 1e-05
MU = 0.9
RATE = 0.7
X, Z, C = 4, 4, 2
Y, H = 4, 2
OFFSETS = (0, 1, 3, 2)
FIRST = (
    (0, (0,), (0, 0), None),
    (0, (1,), (1, 0), None),
    (1, (0,), (2, 0), None),
    (2, (0,), (3, 0), None),
)
SECOND = (
    (0, (2, 3), (0, 0), (1, 4)),
    (0, (0, 1), None, (1, 0)),
    (1, (0,), None, (1, 2)),
    (2, (0,), None, (1, 3)),
)
THIRD = ((1, (1, 2, 3), (0, 0), (1, 0)), (2, (1, 2, 3), (0, 3), (1, 3)))
LAST = ((3, (0, 1), (0, 0), (1, 0)), (3, (2, 3), (2, 0), (3, 0)))
VMEM_LIMIT = 56 * 1024 * 1024
F32 = jnp.float32
BF16 = jnp.bfloat16


def index_of(x, z, c):
    return (x * Z + z) * C + c


def shift(value, dx=0, flip=0, swap=0):
    moves = [
        (index_of(x, z, c), index_of((x + dx) % X, z ^ flip, c ^ swap))
        for x in range(X)
        for z in range(Z)
        for c in range(C)
    ]
    return lax.ppermute(value, "fsdp", moves)


def trade(value, flip=0, far=0):
    moves = [(y * H + h, (y ^ flip) * H + (h ^ far)) for y in range(Y) for h in range(H)]
    return lax.ppermute(value, "replica", moves)


def params(**kw):
    return pltpu.CompilerParams(vmem_limit_bytes=VMEM_LIMIT, **kw)


def norm_kernel(place, acts, gain, cot, rinv, *slots):
    value = acts[...].astype(F32)
    inverse = lax.rsqrt(jnp.mean(value * value, axis=-1, keepdims=True) + EPS)
    rinv[...] = jnp.broadcast_to(inverse, rinv.shape)
    width = acts.shape[1] // X
    span = width // (Z * C)
    for step in range(X):
        base = lax.rem(place[0] + step, X) * width
        for number in range(Z * C):
            core, flip = number // Z, number % Z
            local = (place[1] ^ flip) * (C * span) + (place[2] ^ core) * span
            lanes = pl.ds(pl.multiple_of(base + local, span), span)
            part = acts[:, lanes].astype(F32) * inverse
            slots[step][:, number * span : (number + 1) * span] = (part * gain[:, lanes]).astype(BF16)
        slots[step][:, width:] = cot[...]


def normalise(place, acts, gain, cot):
    tokens, width = acts.shape
    keys = cot.shape[1]
    rows = 64
    part = width // X + keys
    whole = lambda i, place: (0, 0)
    return pl.pallas_call(
        norm_kernel,
        grid_spec=pltpu.PrefetchScalarGridSpec(
            num_scalar_prefetch=1,
            grid=(tokens // rows,),
            in_specs=[
                pl.BlockSpec((rows, width), lambda i, place: (i, 0)),
                pl.BlockSpec((1, width), whole),
                pl.BlockSpec((rows, keys), lambda i, place: (i, 0)),
            ],
            out_specs=[pl.BlockSpec((rows, 128), lambda i, place: (i, 0))]
            + [pl.BlockSpec((rows, part), lambda i, place: (i, 0))] * X,
        ),
        out_shape=[jax.ShapeDtypeStruct((tokens, 128), F32)]
        + [jax.ShapeDtypeStruct((tokens, part), BF16)] * X,
        compiler_params=params(),
        name="normalise",
    )(place, acts, gain, cot)


def pack_kernel(
    r0, r1, r2, r3, second, third, hold, features, rest, base, wide, blocks, early, arrive, leave
):
    tokens = r0.shape[0]
    skip = r0.shape[1] - features.shape[1]
    span = second.shape[0]
    moves = [
        (second, blocks.at[pl.ds(0, span)], rest.at[pl.ds(0, span)]),
        (third, blocks.at[pl.ds(span, third.shape[0])], rest.at[pl.ds(span, third.shape[0])]),
    ]
    moves.append((hold, early, base.at[pl.ds(0, hold.shape[0])]))
    for number, r in enumerate((r0, r1, r2, r3)):
        part = pl.ds(number * tokens, tokens)
        moves.append((r.at[:, pl.ds(skip, features.shape[1])], wide.at[part], features.at[part]))
    loads = [pltpu.make_async_copy(m[0], m[1], arrive.at[i]) for i, m in enumerate(moves)]
    stores = [pltpu.make_async_copy(m[1], m[2], leave.at[i]) for i, m in enumerate(moves)]
    again = pltpu.make_async_copy(
        moves[1][1], base.at[pl.ds(hold.shape[0], third.shape[0])], leave.at[len(moves)]
    )
    for load in loads:
        load.start()
    for load, store in zip(loads, stores):
        load.wait()
        store.start()
    again.start()
    for store in stores + [again]:
        store.wait()


def pack(rows, second, third, hold, span):
    tokens, width = rows[0].shape
    hbm = pl.BlockSpec(memory_space=pl.ANY)
    shapes = [
        (X * tokens, width - Z * span),
        (second.shape[0] + third.shape[0], second.shape[1]),
        (hold.shape[0] + third.shape[0], second.shape[1]),
    ]
    return pl.pallas_call(
        pack_kernel,
        in_specs=[hbm] * (X + 3),
        out_specs=[hbm] * 3,
        out_shape=[jax.ShapeDtypeStruct(shape, BF16) for shape in shapes],
        scratch_shapes=[pltpu.VMEM(shape, BF16) for shape in (*shapes[:2], hold.shape)]
        + [pltpu.SemaphoreType.DMA((X + 3,)), pltpu.SemaphoreType.DMA((X + 4,))],
        compiler_params=params(),
        name="pack",
    )(*rows, second, third, hold)


def wgrad_kernel(r0, r1, r2, r3, other, kept, sent1, sent3):
    span = kept.shape[1]
    own, width = Z * span, Z * C * span
    mine = (r0, r1, r2, r3)
    cots = jnp.concatenate([r[:, width:] for r in mine] + [other[:, own:]], axis=0)
    for flip in range(Z):
        lanes = slice(flip * span, (flip + 1) * span)
        rows = jnp.concatenate([r[:, lanes] for r in mine] + [other[:, lanes]], axis=0)
        total = lax.dot_general(
            rows, cots, (((0,), (0,)), ((), ())), preferred_element_type=F32
        )
        if flip % 2:
            (sent3 if flip == 3 else sent1)[...] = total.astype(BF16)
        else:
            kept[flip // 2] = total


def wgrad_part(rows, other, span, keys):
    vmem = pl.BlockSpec(memory_space=pltpu.VMEM)
    return pl.pallas_call(
        wgrad_kernel,
        in_specs=[vmem] * (X + 1),
        out_specs=[vmem] * 3,
        out_shape=[
            jax.ShapeDtypeStruct((2, span, keys), F32),
            jax.ShapeDtypeStruct((span, keys), BF16),
            jax.ShapeDtypeStruct((span, keys), BF16),
        ],
        compiler_params=params(),
        name="wgrad_part",
    )(*rows, other)


def pieces_of(layout, refs, place, part):
    span = part // (Z * C)
    pieces = []
    for slot, flips, *sources in layout:
        block = lax.rem(place[0] + OFFSETS[slot], X)
        for source, which in zip(sources, (place[2], 1 - place[2])):
            if source is None:
                continue
            number, first = source
            for row, flip in enumerate(flips, first):
                local = pl.multiple_of((place[1] ^ flip) * (C * span) + which * span, span)
                start = pl.multiple_of(block * part + local, span)
                rows = slice(row * span, (row + 1) * span)
                pieces.append((slot, start, local, refs[number], rows))
    return pieces


def keys_sum(pieces, acts, gain, inverse):
    total = None
    for _, start, _, ref, rows in pieces:
        lanes = pl.ds(start, rows.stop - rows.start)
        hat = acts[:, lanes].astype(F32) * inverse
        normed = (hat * gain[:, lanes]).astype(BF16)
        term = jnp.dot(normed, ref[rows, :], preferred_element_type=F32)
        total = term if total is None else total + term
    return total


def cotangent_of(cots, ref, rows):
    return lax.dot_general(
        cots, ref[rows, :], (((1,), (1,)), ((), ())), preferred_element_type=F32
    )


def early_kernel(layout, started, hold, place, acts, gain, rinv, cot, *refs):
    weights, (keys, scaled) = refs[started : -2 - hold], refs[-2 - hold :][:2]
    if hold:
        span = weights[0].shape[0]
        for number, ref in enumerate(weights):
            refs[-1][number * span : (number + 1) * span, :] = ref[...]
    part = acts.shape[1] // X
    inverse = rinv[:, :1]
    pieces = pieces_of(layout, weights, place, part)
    total = keys_sum(pieces, acts, gain, inverse)
    keys[...] = refs[0][...] + total if started else total
    cots = cot[...]
    for number, (_, start, _, ref, rows) in enumerate(pieces):
        span = rows.stop - rows.start
        scaled[number] = inverse * cotangent_of(cots, ref, rows) * gain[:, pl.ds(start, span)]


def backward_early(place, acts, gain, rinv, cot, before, layout, weights, hold=0):
    tokens, width = acts.shape
    span = width // (X * Z * C)
    pieces = sum(len(flips) * (2 - sources.count(None)) for _, flips, *sources in layout)
    vmem = pl.BlockSpec(memory_space=pltpu.VMEM)
    return pl.pallas_call(
        functools.partial(early_kernel, layout, len(before), hold),
        in_specs=[pl.BlockSpec(memory_space=pltpu.SMEM)]
        + [vmem] * (4 + len(before) + len(weights)),
        out_specs=[vmem] * (2 + hold),
        out_shape=[
            jax.ShapeDtypeStruct((tokens, cot.shape[1]), F32),
            jax.ShapeDtypeStruct((pieces, tokens, span), F32),
        ]
        + [jax.ShapeDtypeStruct((len(weights) * span, cot.shape[1]), BF16)] * hold,
        compiler_params=params(),
        name="backward_early",
    )(place, acts, gain, rinv, cot, *before, *weights)


def late_kernel(layout, done, place, acts, gain, rinv, cot, early, *refs):
    sources, refs = refs[: len(done)], refs[len(done) :]
    weights, (keys, dx, held, leave) = refs[:-4], refs[-4:]
    tokens, width = acts.shape
    part = width // X
    inverse = rinv[:, :1]
    pieces = pieces_of(layout, weights, place, part)
    total = early[...] + keys_sum(pieces, acts, gain, inverse)
    keys[...] = total
    cots = cot[...]
    inner = jnp.sum(total * cots.astype(F32), axis=-1, keepdims=True) / width
    factor = rinv[...] * rinv[...] * jnp.broadcast_to(inner, rinv.shape)
    lane = factor.shape[1]
    copies = []

    def send(slot):
        start = pl.multiple_of(lax.rem(place[0] + OFFSETS[slot], X) * part, part)
        lanes = pl.ds(start, part)
        copy = pltpu.make_async_copy(held.at[:, lanes], dx.at[:, lanes], leave.at[slot])
        copy.start()
        copies.append(copy)

    for slot in range(X - 1):
        for source, entries in zip(sources, done):
            for number, (at, start, _, _, rows) in enumerate(
                pieces_of(entries, [None] * 16, place, part)
            ):
                if at != slot:
                    continue
                for first in range(0, rows.stop - rows.start, lane):
                    lanes = pl.ds(pl.multiple_of(start + first, lane), lane)
                    held[:, lanes] = (
                        source[number, :, first : first + lane]
                        - acts[:, lanes].astype(F32) * factor
                    )
        send(slot)
    for slot, start, _, ref, rows in pieces:
        cotangent = cotangent_of(cots, ref, rows)
        for first in range(0, rows.stop - rows.start, lane):
            lanes = pl.ds(pl.multiple_of(start + first, lane), lane)
            held[:, lanes] = (
                rinv[...] * cotangent[:, first : first + lane] * gain[:, lanes]
                - acts[:, lanes].astype(F32) * factor
            )
    send(X - 1)
    for copy in copies:
        copy.wait()


def backward_late(place, acts, gain, rinv, cot, early, sources, done, layout, weights):
    tokens, width = acts.shape
    vmem = pl.BlockSpec(memory_space=pltpu.VMEM)
    return pl.pallas_call(
        functools.partial(late_kernel, layout, done),
        in_specs=[pl.BlockSpec(memory_space=pltpu.SMEM)]
        + [vmem] * (5 + len(sources) + len(weights)),
        out_specs=[vmem, pl.BlockSpec(memory_space=pl.ANY)],
        out_shape=[
            jax.ShapeDtypeStruct((tokens, cot.shape[1]), F32),
            jax.ShapeDtypeStruct((tokens, width), F32),
        ],
        scratch_shapes=[pltpu.VMEM((tokens, width), F32), pltpu.SemaphoreType.DMA((X,))],
        compiler_params=params(),
        name="backward_late",
    )(place, acts, gain, rinv, cot, early, *sources, *weights)


def delta_kernel(place, glob, local, keep, send):
    rows = keep.shape[1]
    for flip, out, row in ((0, keep, 0), (3, keep, 1), (1, send, 0), (2, send, 1)):
        part = pl.ds(pl.multiple_of((place[3] ^ flip) * rows, rows), rows)
        out[row] = glob[part, :] - local[part, :]


def delta(place, glob, local):
    rows, width = glob.shape
    vmem = pl.BlockSpec(memory_space=pltpu.VMEM)
    return pl.pallas_call(
        delta_kernel,
        in_specs=[pl.BlockSpec(memory_space=pltpu.SMEM), vmem, vmem],
        out_specs=[vmem, vmem],
        out_shape=[jax.ShapeDtypeStruct((2, rows // Y, width), F32)] * 2,
        compiler_params=params(),
        name="delta",
    )(place, glob, local)


def outer_kernel(place, p03, p12, glob, codes, scales, new_global, new_codes, new_scales):
    rows = p03.shape[1]
    blocks = scales.shape[0]
    span = p03.shape[2] // blocks
    columns = jnp.concatenate([scales[...]] * (128 // blocks), axis=0).T
    spread = 128 // blocks
    for flip, part in ((0, p03.at[0]), (3, p03.at[1]), (1, p12.at[0]), (2, p12.at[1])):
        start = pl.multiple_of((place[3] ^ flip) * rows, rows)
        new_global[pl.ds(start, rows), :] = part[...]
    maxima = []
    for block in range(blocks):
        lanes = slice(block * span, (block + 1) * span)
        pseudo = new_global[:, lanes]
        momentum = codes[:, lanes].astype(F32) * columns[:, block : block + 1]
        moved = MU * momentum + pseudo
        new_global[:, lanes] = glob[:, lanes] - RATE * (pseudo + MU * moved)
        scale = jnp.max(jnp.abs(moved), axis=-1, keepdims=True) + 1e-06
        new_codes[:, lanes] = (moved / scale).astype(BF16)
        maxima.append(jnp.broadcast_to(scale, (Y * rows, spread)))
    across = jnp.concatenate(maxima, axis=-1).T
    new_scales[...] = jnp.concatenate(
        [across[start : start + 1] for start in range(0, 128, spread)], axis=0
    )


def outer_update(place, p03, p12, glob, codes, scales):
    vmem = pl.BlockSpec(memory_space=pltpu.VMEM)
    new_global, new_codes, new_scales = pl.pallas_call(
        outer_kernel,
        in_specs=[pl.BlockSpec(memory_space=pltpu.SMEM)] + [vmem] * 5,
        out_specs=[vmem] * 3,
        out_shape=[
            jax.ShapeDtypeStruct(glob.shape, F32),
            jax.ShapeDtypeStruct(codes.shape, BF16),
            jax.ShapeDtypeStruct(scales.shape[::-1], F32),
        ],
        compiler_params=params(),
        name="outer_update",
    )(place, p03, p12, glob, codes, scales.T)
    return new_global, new_codes, new_scales.T


def together(*values):
    return lax.optimization_barrier(values)


def body(
    activations,
    norm_gain,
    key_weight,
    key_cotangent,
    local_fragment,
    global_fragment,
    momentum_codes,
    momentum_scales,
):
    acts, weight, cot = activations[0], key_weight[0], key_cotangent[0]
    here, replica = lax.axis_index("fsdp"), lax.axis_index("replica")
    place = jnp.stack([here // (Z * C), (here // C) % Z, here % C, replica // H]).astype(jnp.int32)
    span = weight.shape[0]

    width = cot.shape[1]
    second = shift(weight, flip=1)
    near3, near1 = shift(weight, dx=1), shift(weight, dx=-1)
    keep, send = delta(place, global_fragment, local_fragment[0])
    came = trade(send, flip=1)
    rinv, *slots = normalise(place, acts, norm_gain, cot)
    gain_here = lax.dynamic_slice_in_dim(norm_gain[0], here * span, span)
    ratio = weight.astype(F32) / gain_here[:, None]
    *slots, second, near3, near1, came, ratio = together(
        *slots, second, near3, near1, came, ratio
    )

    rows = [slots[0]] + [shift(slots[d], dx=d) for d in (1, 3, 2)]
    third = shift(jnp.concatenate([weight, second], axis=0), flip=2)
    keep = keep + came
    total = keep[0] + trade(keep[1], flip=3)
    came = trade(total, far=1)
    early, first, hold = backward_early(
        place, acts, norm_gain, rinv, cot, (), FIRST, (weight, second, near1, near3), hold=1
    )
    *rows, third, came, early = together(*rows, third, came, early)
    pseudo = (total + came) / (Y * H)

    other, rest, base = pack(rows, second, third, hold, span)
    other = shift(other, swap=1)
    far3, far1 = shift(rest, dx=1), shift(rest, dx=-1)
    came = trade(pseudo, flip=3)
    other, came = together(other, came)
    p03 = jnp.stack([pseudo, came])
    p12 = trade(p03, flip=1)
    kept, sent1, sent3 = wgrad_part(rows, other, span, width)
    base_mate = shift(base, swap=1)
    early, sent1 = together(early, sent1)
    early, second_part = backward_early(
        place, acts, norm_gain, rinv, cot, (early,), SECOND, (third, base_mate)
    )
    back3 = shift(sent3, flip=1)
    far3, far1, early, back3, p12 = together(far3, far1, early, back3, p12)

    across_a = shift(jnp.concatenate([near1, far1[:span]], axis=0), dx=-1)
    across_b = shift(far3[span:], dx=1)
    far = jnp.concatenate([far1, far3], axis=0)
    far_mate = shift(far, swap=1)
    last = (kept[1] + back3.astype(F32)).astype(BF16)
    end = shift(last, flip=2)
    back1 = shift(sent1, flip=1)
    early, third_part = backward_early(
        place, acts, norm_gain, rinv, cot, (early,), THIRD, (far, far_mate)
    )
    early, end, back1 = together(early, end, back1)
    weight_grad = kept[0] + back1.astype(F32) + end.astype(F32)
    gain_grad = jnp.sum(ratio * weight_grad, axis=-1)
    new_global, new_codes, new_scales = outer_update(
        place, p03, p12, global_fragment, momentum_codes, momentum_scales
    )
    across_a, across_b, early, gain_grad, new_scales = together(
        across_a, across_b, early, gain_grad, new_scales
    )
    mate_a, mate_b = shift(across_a, swap=1), shift(across_b, swap=1)
    keys, input_gradient_rows = backward_late(
        place, acts, norm_gain, rinv, cot, early, (first, second_part, third_part),
        (FIRST, SECOND, THIRD), LAST, (across_a, mate_a, across_b, mate_b),
    )
    return (
        keys[None],
        weight_grad[None],
        gain_grad[None],
        input_gradient_rows[None],
        new_global,
        new_codes,
        new_scales,
    )


def solution(mesh):
    in_specs = (
        P("replica", "fsdp", None),
        P("replica", None),
        P("replica", "fsdp", None),
        P("replica", "fsdp", None),
        P("replica", "fsdp", None),
        P("fsdp", None),
        P("fsdp", None),
        P("fsdp", None),
    )
    out_specs = (
        P("replica", "fsdp", None),
        P("replica", "fsdp", None),
        P("replica", "fsdp"),
        P("replica", "fsdp", None),
        P("fsdp", None),
        P("fsdp", None),
        P("fsdp", None),
    )
    return jax.shard_map(body, mesh=mesh, in_specs=in_specs, out_specs=out_specs, check_vma=False)
```
